768 devices in a mesh: prow: 96 (over z, x, core), pcol: 8 (over y).
Axes of the slice: x: 4, y: 8, z: 12, core: 2. Of those that a mesh axis runs over, the one named last changes fastest.
Arguments:
- dof_values: float32 [9, 56, 98304], P(None, None, ('prow', 'pcol')), may hold values from -6 to 6
- grad_matrix: float32 [3, 56, 56], replicated, may hold values from -0.75 to 0.75
- stiff_matrix: float32 [3, 56, 56], replicated, may hold values from -0.1875 to 0.1875
- face_proj: float32 [4, 21, 56], replicated, may hold values from -0.75 to 0.75
- face_lift: float32 [4, 56, 21], replicated, may hold values from -0.3125 to 0.3125
- rotate: float32 [3, 21, 21], replicated, may hold values from -1.25 to 1.25
- material: float32 [16, 3], replicated, may hold values from 0.5 to 2
- material_id: int32 [98304], P(('prow', 'pcol')), may hold values from 0 to 15
- inv_jacobian: float32 [3, 3, 98304], P(None, None, ('prow', 'pcol')), may hold values from -3 to 3
- normals: float32 [4, 3, 98304], P(None, None, ('prow', 'pcol')), may hold values from -2 to 2
- orientation: int32 [4, 98304], P(None, ('prow', 'pcol')), may hold values from 0 to 2
- neighbour: int32 [4, 98304], P(None, ('prow', 'pcol')), may hold values from -1 to 127, as said below
- neighbour_face: int32 [4, 98304], P(None, ('prow', 'pcol')), may hold values from 0 to 3, as said below
- send_list: int32 [96, 8, 8, 24], P('prow', 'pcol'), may hold values from -1 to 511, as said below
- recv_list: int32 [96, 8, 8, 24], P('prow', 'pcol'), may hold values from -1 to 511, as said below
Outputs:
- new_dofs: float32 [9, 56, 98304], P(None, None, ('prow', 'pcol'))
The draws below stay inside these ranges and needn't reach their ends.
Inputs may be any that keep to these rules, and one draw needn't show every extreme that they name: `neighbour`: -1 where the face has no neighbour in the same partition; otherwise faces are matched in pairs: the element neighbour[f, e] lists e back across its face neighbour_face[f, e]. `neighbour_face`: 0 where neighbour is -1. `send_list`: entry (r, c, d, m) is a local face id of partition (r, c) whose neighbour lies in the partition at offset d, or -1; live slots of a direction come first, each such face appears once, and the live count of (r, c, d) equals that of the partner's direction 7 - d; directions leaving the grid have none. Some partition has 24 live slots in all eight directions, and every live count is at most 24. `recv_list`: entry (r, c, d, m) is the local face id of partition (r, c) that meets the face in slot m of the send_list of the partner at offset d for direction 7 - d, or -1 where that slot is empty; its live slots hold the same faces as send_list of (r, c, d) in another order.
All inputs are finite; a program needn't handle non-finite values.
Results may differ from the reference program's by a relative error of at most 0.0003.
Values sent between devices are 32-bit elements; how exact they have to be, the bound alone decides.
A program may use at most 32 MiB of HBM per device.

```python
import math
import jax
import jax.numpy as jnp
from jax import lax

BASIS = 56
FACE_BASIS = 21
QUANT = 9
ORDER = 6
STEPS = 2
MATERIALS = 16
E_DEV = 128
PEER_CAP = 24
E = 98304
N_PROW = 96
N_PCOL = 8


OFFSETS = ((-1, -1), (-1, 0), (-1, 1), (0, -1), (0, 1), (1, -1), (1, 0), (1, 1))


def link_tables(key):
    row_count = N_PROW
    col_count = N_PCOL
    face_count = 4 * E_DEV
    devices = row_count * col_count
    key = jax.random.fold_in(key, 9173)
    key_count, key_turn, key_hub_row, key_hub_col, key_perm = jax.random.split(key, 5)
    link_raw = jax.random.randint(key_count, (row_count, col_count, 8), (PEER_CAP + 3) // 4, PEER_CAP + 1)
    turn_raw = jax.random.randint(key_turn, (row_count, col_count, 8), 0, PEER_CAP)
    hub_row = jax.random.randint(key_hub_row, (), 1, row_count - 1)
    hub_col = jax.random.randint(key_hub_col, (), 1, col_count - 1)
    row_ids = jnp.arange(row_count, dtype=jnp.int32)[:, None]
    col_ids = jnp.arange(col_count, dtype=jnp.int32)[None, :]
    link_planes = []
    for direction in range(8):
        link_plane = link_raw[:, :, direction]
        if direction >= 4:
            row_step, col_step = OFFSETS[direction]
            at_hub = (row_ids == hub_row) & (col_ids == hub_col)
            before_hub = (row_ids == hub_row - row_step) & (col_ids == hub_col - col_step)
            link_plane = jnp.where(at_hub | before_hub, PEER_CAP, link_plane)
        link_planes.append(link_plane)
    counts = []
    turns = []
    for direction in range(8):
        row_step, col_step = OFFSETS[direction]
        inside = (row_ids + row_step >= 0) & (row_ids + row_step < row_count) & (col_ids + col_step >= 0) & (col_ids + col_step < col_count)
        if direction >= 4:
            link_count = link_planes[direction]
            link_turn = -turn_raw[:, :, direction]
        else:
            link_count = jnp.roll(link_planes[7 - direction], (-row_step, -col_step), (0, 1))
            link_turn = jnp.roll(turn_raw[:, :, 7 - direction], (-row_step, -col_step), (0, 1))
        counts.append(jnp.where(inside, link_count, 0))
        turns.append(link_turn)
    counts = jnp.stack(counts, axis=2).reshape(devices, 8)
    turns = jnp.stack(turns, axis=2).reshape(devices, 8)
    device_keys = jax.random.split(key_perm, devices)
    face_order = jax.vmap(lambda dev_key: jax.random.permutation(dev_key, face_count))(device_keys).astype(jnp.int32)
    starts = jnp.cumsum(counts, axis=1) - counts
    boundary = jnp.sum(counts, axis=1)
    slot_ids = jnp.arange(PEER_CAP, dtype=jnp.int32)
    live_slot = slot_ids[None, None, :] < counts[:, :, None]
    places = jnp.minimum(starts[:, :, None] + slot_ids[None, None, :], face_count - 1).reshape(devices, 8 * PEER_CAP)
    send_table = jnp.take_along_axis(face_order, places, axis=1).reshape(devices, 8, PEER_CAP)
    send_table = jnp.where(live_slot, send_table, -1)
    live_span = jnp.maximum(counts, 1)[:, :, None]
    source = (slot_ids[None, None, :] + turns[:, :, None]) % live_span
    recv_table = jnp.take_along_axis(send_table, source, axis=2)
    recv_table = jnp.where(live_slot, recv_table, -1)
    positions = jnp.arange(face_count, dtype=jnp.int32)[None, :]
    partner = boundary[:, None] + jnp.bitwise_xor(positions - boundary[:, None], 1)
    paired = (positions >= boundary[:, None]) & (partner < face_count)
    partner_face = jnp.take_along_axis(face_order, jnp.clip(partner, 0, face_count - 1), axis=1)
    near_elem = jnp.where(paired, partner_face % E_DEV, -1)
    near_face = jnp.where(paired, partner_face // E_DEV, 0)
    neighbour_table = jax.vmap(lambda where_ids, vals: jnp.zeros((face_count,), jnp.int32).at[where_ids].set(vals))(face_order, near_elem)
    near_face_table = jax.vmap(lambda where_ids, vals: jnp.zeros((face_count,), jnp.int32).at[where_ids].set(vals))(face_order, near_face)
    neighbour_table = jnp.transpose(neighbour_table.reshape(devices, 4, E_DEV), (1, 0, 2)).reshape(4, devices * E_DEV)
    near_face_table = jnp.transpose(near_face_table.reshape(devices, 4, E_DEV), (1, 0, 2)).reshape(4, devices * E_DEV)
    send_table = send_table.reshape(row_count, col_count, 8, PEER_CAP)
    recv_table = recv_table.reshape(row_count, col_count, 8, PEER_CAP)
    return (neighbour_table, near_face_table, send_table, recv_table)


def draw_neighbour(key, part):
    return link_tables(key)[0]


def draw_neighbour_face(key, part):
    return link_tables(key)[1]


def draw_send_list(key, part):
    return link_tables(key)[2]


def draw_recv_list(key, part):
    return link_tables(key)[3]


def plant(values, stream_key, low, largest):
    dims = values.shape
    place = [jax.random.randint(jax.random.fold_in(stream_key, axis), (), 0, dims[axis]) for axis in range(len(dims))]
    values = values.at[tuple(place)].set(low)
    longest = dims.index(max(dims))
    place[longest] = (place[longest] + 1) % dims[longest]
    return values.at[tuple(place)].set(largest)


def shard_levels(stream_key, shape, cuts, low, largest):
    gain = 1.0
    for axis_at, shards_of in cuts:
        heights = jax.random.uniform(jax.random.fold_in(jax.random.fold_in(stream_key, 6), axis_at), (shards_of,), jnp.float32, low / len(cuts), largest / len(cuts))
        gain = gain * jnp.repeat(jnp.exp(heights), shape[axis_at] // shards_of).reshape((-1,) + (1,) * (len(shape) - 1 - axis_at))
    return gain


def centred(stream_key, dims, width, limit, shards=(), kind=jnp.bfloat16):
    values = jax.random.normal(stream_key, dims, jnp.float32) * width
    if len(shards) > 0:
        values = shard_levels(stream_key, dims, shards, -0.22, 0.18) * values
    return jnp.clip(values, min=-limit, max=limit).astype(kind)


def setup_inputs(seed: int = 0) -> dict:
    key_list = jax.random.split(jax.random.key(seed), 16)
    return {
        "dof_values": centred(key_list[0], (QUANT, BASIS, E), 1.0, 6.0, ((2, 768),), jnp.float32),
        "grad_matrix": centred(key_list[1], (3, BASIS, BASIS), BASIS ** -0.5, 0.75, (), jnp.float32),
        "stiff_matrix": centred(key_list[2], (3, BASIS, BASIS), (16 * BASIS) ** -0.5, 0.1875, (), jnp.float32),
        "face_proj": centred(key_list[3], (4, FACE_BASIS, BASIS), BASIS ** -0.5, 0.75, (), jnp.float32),
        "face_lift": centred(key_list[4], (4, BASIS, FACE_BASIS), (16 * FACE_BASIS) ** -0.5, 0.3125, (), jnp.float32),
        "rotate": centred(key_list[5], (3, FACE_BASIS, FACE_BASIS), FACE_BASIS ** -0.5, 1.25, (), jnp.float32),
        "material": jnp.clip(jnp.exp(jax.random.uniform(key_list[6], (MATERIALS, 3), jnp.float32, math.log(0.5), math.log(2.0))), 0.5, 2.0),
        "material_id": plant(jax.random.randint(key_list[7], (E,), 0, MATERIALS), jax.random.fold_in(key_list[7], 1), 0, MATERIALS - 1).astype(jnp.int32),
        "inv_jacobian": centred(key_list[8], (3, 3, E), 0.5, 3.0, ((2, 768),), jnp.float32),
        "normals": centred(key_list[9], (4, 3, E), 0.3, 2.0, ((2, 768),), jnp.float32),
        "orientation": plant(jax.random.randint(key_list[10], (4, E), 0, 3), jax.random.fold_in(key_list[10], 1), 0, 2).astype(jnp.int32),
        "neighbour": draw_neighbour(jax.random.fold_in(key_list[15], 71), 0),
        "neighbour_face": draw_neighbour_face(jax.random.fold_in(key_list[15], 71), 0),
        "send_list": draw_send_list(jax.random.fold_in(key_list[15], 71), 0),
        "recv_list": draw_recv_list(jax.random.fold_in(key_list[15], 71), 0),
    }


exact_mode = lax.Precision.HIGHEST
time_step = 0.8
OFFSETS = ((-1, -1), (-1, 0), (-1, 1), (0, -1), (0, 1), (1, -1), (1, 0), (1, 1))
ENTRIES = ((0, 0, 6, 0), (0, 1, 6, 1), (0, 2, 6, 1), (0, 3, 7, 2), (0, 5, 8, 2), (0, 6, 0, 3), (0, 7, 3, 3), (0, 8, 5, 3), (1, 0, 7, 1), (1, 1, 7, 0), (1, 2, 7, 1), (1, 3, 6, 2), (1, 4, 8, 2), (1, 6, 3, 3), (1, 7, 1, 3), (1, 8, 4, 3), (2, 0, 8, 1), (2, 1, 8, 1), (2, 2, 8, 0), (2, 4, 7, 2), (2, 5, 6, 2), (2, 6, 5, 3), (2, 7, 4, 3), (2, 8, 2, 3))

def element_params(material, material_id, normals):
    id_range = jnp.arange(material.shape[0], dtype=jnp.int32)
    onehot = (material_id[None, :] == id_range[:, None]).astype(material.dtype)
    params = jnp.dot(material.T, onehot, precision=exact_mode)
    density, lame_first, shear_modulus = (params[0], params[1], params[2])
    values = (-(lame_first + 2.0 * shear_modulus), -lame_first, -shear_modulus, -1.0 / density)
    wave_speed = jnp.sqrt((lame_first + 2.0 * shear_modulus) / density) * lax.optimization_barrier(jnp.sum(jnp.abs(normals), axis=1))
    return (values, wave_speed)

def elastic_apply(parts, values):
    result = [None] * 9
    for comp_axis, row_index, col_index, kind_index in ENTRIES:
        term = values[kind_index] * parts[comp_axis][col_index]
        result[row_index] = term if result[row_index] is None else result[row_index] + term
    return jnp.stack(result, axis=0)

def star_apply(slopes, inv_jacobian, values):
    parts = [lax.optimization_barrier(jnp.sum(inv_jacobian[:, k][:, None, None, :] * slopes, axis=0)) for k in range(3)]
    return elastic_apply(parts, values)

def predict(current, inv_jacobian, values, grad_matrix):
    derivative = current
    integrated = time_step * current
    factor = time_step
    for power_level in range(1, ORDER):
        slopes = jnp.einsum('dab,qbe->dqae', grad_matrix, derivative, precision=exact_mode)
        derivative = -star_apply(slopes, inv_jacobian, values)
        factor = factor * time_step / (power_level + 1)
        integrated = integrated + factor * derivative
    return integrated

def local_part(current, inv_jacobian, values, grad_matrix, stiff_matrix, face_proj):
    integrated = predict(current, inv_jacobian, values, grad_matrix)
    slopes = jnp.einsum('dab,qbe->dqae', stiff_matrix, integrated, precision=exact_mode)
    volume = star_apply(slopes, inv_jacobian, values)
    face_data = jnp.einsum('fib,qbe->qife', face_proj, integrated, precision=exact_mode)
    return (volume, face_data)

def face_update(current, volume, face_data, neighbour_data, orientation, normals, values, wave_speed, rotate, face_lift):
    turned = jnp.einsum('hil,qlfe->hqife', rotate, neighbour_data, precision=exact_mode)
    chosen = (orientation[None] == jnp.arange(3, dtype=jnp.int32)[:, None, None]).astype(current.dtype)
    turned = lax.optimization_barrier(jnp.sum(turned * chosen[:, None, None, :, :], axis=0))
    both = face_data + turned
    apart = face_data - turned
    parts = [normals[:, k, :][None, None] * both for k in range(3)]
    flux_total = 0.5 * (elastic_apply(parts, values) + wave_speed[None, None] * apart)
    lifted = jnp.einsum('fai,pife->pae', face_lift, flux_total, precision=exact_mode)
    return current + volume - lifted

def reference(dof_values, grad_matrix, stiff_matrix, face_proj, face_lift, rotate, material, material_id, inv_jacobian, normals, orientation, neighbour, neighbour_face, send_list, recv_list):
    devices = N_PROW * N_PCOL

    def blocks(array):
        return jnp.moveaxis(array.reshape(array.shape[:-1] + (devices, E_DEV)), -2, 0)
    current = blocks(dof_values)
    mat_blocks = blocks(material_id)
    jac_blocks = blocks(inv_jacobian)
    normal_blocks = blocks(normals)
    orient_blocks = blocks(orientation)
    near_blocks = blocks(neighbour)
    near_face_blocks = blocks(neighbour_face)
    send_all = send_list.reshape(devices, 8, PEER_CAP)
    recv_all = recv_list.reshape(devices, 8, PEER_CAP)
    block_ids = jnp.arange(devices, dtype=jnp.int32)

    def block_local(inputs):
        block_state, block_material, block_jac, block_normals = inputs
        values, wave_speed = element_params(material, block_material, block_normals)
        return local_part(block_state, block_jac, values, grad_matrix, stiff_matrix, face_proj)
    for time_index in range(STEPS):
        volume, face_data = lax.map(block_local, (current, mat_blocks, jac_blocks, normal_blocks))
        flat_faces = face_data.reshape(devices, 9, FACE_BASIS, 4 * E_DEV)

        def block_update(inputs):
            block_id, block_state, block_volume, block_material, block_normals, block_orient, block_near, block_near_face, block_recv = inputs
            values, wave_speed = element_params(material, block_material, block_normals)
            own_faces = flat_faces[block_id]
            local_index = (block_near_face * E_DEV + jnp.maximum(block_near, 0)).reshape(-1)
            local_data = jnp.take(own_faces, local_index, axis=2)
            pieces = []
            for direction in range(8):
                row_step, col_step = OFFSETS[direction]
                partner = jnp.clip(block_id + row_step * N_PCOL + col_step, 0, devices - 1)
                source_ids = send_all[partner, 7 - direction]
                sent_data = jnp.take(flat_faces[partner], jnp.maximum(source_ids, 0), axis=2)
                pieces.append(sent_data * (source_ids >= 0).astype(own_faces.dtype))
            received = jnp.concatenate(pieces, axis=2)
            targets = jnp.where(block_recv >= 0, block_recv, 4 * E_DEV).reshape(-1)
            arrived = jnp.zeros_like(own_faces).at[:, :, targets].set(received, mode='drop')
            inside = (block_near >= 0).reshape(-1)
            neighbour_data = jnp.where(inside, local_data, arrived).reshape(9, FACE_BASIS, 4, E_DEV)
            own_data = own_faces.reshape(9, FACE_BASIS, 4, E_DEV)
            return face_update(block_state, block_volume, own_data, neighbour_data, block_orient, block_normals, values, wave_speed, rotate, face_lift)
        current = lax.map(block_update, (block_ids, current, volume, mat_blocks, normal_blocks, orient_blocks, near_blocks, near_face_blocks, recv_all))
    return jnp.moveaxis(current, 0, -2).reshape(dof_values.shape)
```

```python
import functools

import jax
import jax.numpy as jnp
from jax import lax
from jax.experimental import pallas as pl
from jax.experimental.pallas import tpu as pltpu
from jax.sharding import PartitionSpec as P

ORDER = 6
STEPS = 2
TIME_STEP = 0.8
OFFSETS = ((-1, -1), (-1, 0), (-1, 1), (0, -1), (0, 1), (1, -1), (1, 0), (1, 1))
MESH = pl.DeviceIdType.MESH
F32 = jnp.float32
BF16 = jnp.bfloat16
QUANT = 9
BASIS = 56
KBLOCK = 64
FACE = 21
FROWS = 24
ELEMS = 128
FACES = 4 * ELEMS
SLOTS = 24
WIDE = 256


def dot(a, b):
    return lax.dot_general(a, b, (((1,), (0,)), ((), ())), preferred_element_type=F32)


def dot_nt(a, b):
    return lax.dot_general(a, b, (((1,), (1,)), ((), ())), preferred_element_type=F32)


def low_of(x):
    return x - x.astype(BF16).astype(F32)


def widen(x, rows):
    if x.shape[0] == rows:
        return x
    return jnp.concatenate([x, jnp.zeros((rows - x.shape[0], x.shape[1]), F32)], axis=0)


def stacked(slabs, rows):
    columns = []
    for slab in slabs:
        full = widen(slab, rows)
        high = full.astype(BF16)
        low = (full - high.astype(F32)).astype(BF16)
        columns.append(jnp.concatenate([high, high, low], axis=0))
    return jnp.concatenate(columns, axis=1)


def stress_rates(ux, vy, wz, uv, vw, uw, lame, shear2, shear):
    spread = lame * (ux + vy + wz)
    return [
        spread + shear2 * ux,
        spread + shear2 * vy,
        spread + shear2 * wz,
        shear * uv,
        shear * vw,
        shear * uw,
    ]


def kernel(
    rows,
    cols,
    dof_ref,
    grad_ref,
    stiff_ref,
    proj_ref,
    lift_ref,
    rot_ref,
    mat_ref,
    mid_ref,
    jac_ref,
    nrm_ref,
    ori_ref,
    near_ref,
    near_face_ref,
    send_list_ref,
    recv_list_ref,
    out_ref,
    tmp,
    grad_w,
    stiff_w,
    proj_w,
    lift_w,
    rot_w,
    near_w,
    give_w,
    take_w,
    send_buf,
    recv_buf,
    send_sem,
    recv_sem,
):
    row = lax.axis_index("prow")
    col = lax.axis_index("pcol")
    partners = [
        (lax.rem(row + (dr + rows), rows), lax.rem(col + (dc + cols), cols)) for dr, dc in OFFSETS
    ]
    barrier = pltpu.get_barrier_semaphore()
    for partner in partners:
        pl.semaphore_signal(barrier, inc=1, device_id=partner, device_id_type=MESH)

    def split_store(dest, at, block, step_k, first=True):
        height, width = block.shape
        dest[at : at + height, 0:width] = block
        dest[at : at + height, step_k : step_k + width] = low_of(block)
        dest[at : at + height, 2 * step_k : 2 * step_k + width] = block

    tmp[...] = jnp.zeros_like(tmp)
    for d in range(3):
        split_store(tmp, d * BASIS, grad_ref[d], KBLOCK)
    grad_w[...] = tmp[0:176, 0 : 3 * KBLOCK].astype(BF16)
    for d in range(3):
        split_store(tmp, d * BASIS, stiff_ref[d], KBLOCK)
    stiff_w[...] = tmp[0:176, 0 : 3 * KBLOCK].astype(BF16)
    tmp[...] = jnp.zeros_like(tmp)
    for f in range(4):
        split_store(tmp, f * FROWS, proj_ref[f], KBLOCK)
    proj_w[...] = tmp[0:96, 0 : 3 * KBLOCK].astype(BF16)
    tmp[...] = jnp.zeros_like(tmp)
    for h in range(3):
        split_store(tmp, h * FROWS, rot_ref[h], FROWS)
    rot_w[...] = tmp[0:80, 0:80].astype(BF16)
    tmp[...] = jnp.zeros_like(tmp)
    for f in range(4):
        block = lift_ref[f]
        tmp[0:BASIS, f * FROWS : f * FROWS + FACE] = block
        tmp[0:BASIS, 96 + f * FROWS : 96 + f * FROWS + FACE] = low_of(block)
        tmp[0:BASIS, 192 + f * FROWS : 192 + f * FROWS + FACE] = block
    lift_w[...] = tmp[0:64, 0:288].astype(BF16)

    face_rows = lax.broadcasted_iota(jnp.int32, (FACES, ELEMS), 0)
    for f in range(4):
        near = near_ref[f : f + 1, :]
        source = jnp.where(near >= 0, near_face_ref[f : f + 1, :] * ELEMS + near, -1)
        near_w[:, f * ELEMS : (f + 1) * ELEMS] = (face_rows == source).astype(F32).astype(BF16)
    outside = jnp.concatenate([near_ref[f : f + 1, :] < 0 for f in range(4)], axis=1)
    face_ids = lax.broadcasted_iota(jnp.int32, (SLOTS, FACES), 1)
    give_ids = jnp.transpose(send_list_ref[0, 0])
    take_ids = jnp.transpose(recv_list_ref[0, 0])
    give_parts = []
    take_parts = []
    for d in range(8):
        give_parts.append((give_ids[:, d : d + 1] == face_ids).astype(F32))
        take_parts.append(
            jnp.where((take_ids[:, d : d + 1] == face_ids) & outside, 1.0, 0.0).astype(F32)
        )
    give_w[...] = jnp.concatenate(give_parts, axis=0).astype(BF16)
    take_w[...] = jnp.concatenate(take_parts, axis=0).astype(BF16)

    hot = lax.broadcasted_iota(jnp.int32, (16, ELEMS), 0) == mid_ref[...]
    density, lame, shear = [
        jnp.sum(jnp.where(hot, mat_ref[:, j : j + 1], 0.0), axis=0, keepdims=True) for j in range(3)
    ]
    inverse = 1.0 / density
    jac = [[jac_ref[d, k : k + 1, :] for k in range(3)] for d in range(3)]
    root = jnp.sqrt((lame + 2.0 * shear) * inverse)
    orient = jnp.concatenate([ori_ref[f : f + 1, :] for f in range(4)], axis=1)

    def along(slopes, columns):
        def one(place, k):
            parts = [
                jac[d][k]
                * slopes[d * BASIS : (d + 1) * BASIS, place * ELEMS : (place + 1) * ELEMS]
                for d in range(3)
            ]
            return parts[0] + parts[1] + parts[2]

        return one

    def stress_from(slopes, scale):
        one = along(slopes, 3)
        ux, vy, wz = one(0, 0), one(1, 1), one(2, 2)
        uv = one(1, 0) + one(0, 1)
        vw = one(2, 1) + one(1, 2)
        uw = one(2, 0) + one(0, 2)
        return stress_rates(
            ux, vy, wz, uv, vw, uw, scale * lame, (2.0 * scale) * shear, scale * shear
        )

    def speed_from(slopes, scale):
        one = along(slopes, 6)
        over = scale * inverse
        return [
            over * (one(0, 0) + one(3, 1) + one(5, 2)),
            over * (one(3, 0) + one(1, 1) + one(4, 2)),
            over * (one(5, 0) + one(4, 1) + one(2, 2)),
        ]

    for step in range(STEPS):
        current = dof_ref if step == 0 else out_ref
        level = [TIME_STEP * current[q] for q in range(QUANT)]
        total = list(level)
        for power in range(1, ORDER):
            scale = TIME_STEP / (power + 1)
            from_stress = dot(grad_w[...], stacked(level[:6], KBLOCK))
            from_speed = dot(grad_w[...], stacked(level[6:], KBLOCK))
            level = stress_from(from_speed, scale) + speed_from(from_stress, scale)
            total = [t + x for t, x in zip(total, level)]

        whole = stacked(total, KBLOCK)
        own = dot(proj_w[...], whole)
        faces = jnp.concatenate(
            [
                jnp.concatenate(
                    [
                        own[f * FROWS : (f + 1) * FROWS, q * ELEMS : (q + 1) * ELEMS]
                        for f in range(4)
                    ],
                    axis=1,
                )
                for q in range(QUANT)
            ]
            + [jnp.zeros((WIDE - QUANT * FROWS, FACES), F32)],
            axis=0,
        )
        faces_high = faces.astype(BF16)
        faces_low = (faces - faces_high.astype(F32)).astype(BF16)
        outgoing = dot_nt(give_w[...], faces_high) + dot_nt(give_w[...], faces_low)
        for d in range(8):
            send_buf[step, d] = outgoing[d * SLOTS : (d + 1) * SLOTS]
        if step == 0:
            pl.semaphore_wait(barrier, 8)
        copies = []
        for d in range(8):
            copy = pltpu.make_async_remote_copy(
                src_ref=send_buf.at[step, d],
                dst_ref=recv_buf.at[step, 7 - d],
                send_sem=send_sem.at[step, d],
                recv_sem=recv_sem.at[step, 7 - d],
                device_id=partners[d],
                device_id_type=MESH,
            )
            copy.start()
            copies.append(copy)

        slopes = dot(stiff_w[...], whole)
        volume = stress_from(slopes[:, 6 * ELEMS :], -1.0) + speed_from(slopes[:, : 6 * ELEMS], -1.0)
        for q in range(QUANT):
            out_ref[q] = current[q] + volume[q]
        beside = dot(faces_high, near_w[...]) + dot(faces_low, near_w[...])

        for copy in copies:
            copy.wait_recv()
        got = jnp.transpose(
            jnp.concatenate([recv_buf[step, d] for d in range(8)], axis=0)
        )
        got_high = got.astype(BF16)
        got_low = (got - got_high.astype(F32)).astype(BF16)
        beside = beside + dot(got_high, take_w[...]) + dot(got_low, take_w[...])

        turned = []
        for q in range(QUANT):
            block = beside[q * FROWS : (q + 1) * FROWS]
            low = low_of(block)
            right = jnp.concatenate([block, block, low, jnp.zeros((8, FACES), F32)], axis=0)
            each = dot(rot_w[...], right.astype(BF16))
            turned.append(
                jnp.where(
                    orient == 0,
                    each[0:FROWS],
                    jnp.where(orient == 1, each[FROWS : 2 * FROWS], each[2 * FROWS : 3 * FROWS]),
                )
            )

        fluxes = [[] for _ in range(QUANT)]
        for f in range(4):
            here = slice(f * ELEMS, (f + 1) * ELEMS)
            n = [nrm_ref[f, k : k + 1, :] for k in range(3)]
            both = []
            apart = []
            for q in range(QUANT):
                mine = own[f * FROWS : (f + 1) * FROWS, q * ELEMS : (q + 1) * ELEMS]
                theirs = turned[q][:, here]
                both.append(mine + theirs)
                apart.append(mine - theirs)
            half = 0.5 * root * (jnp.abs(n[0]) + jnp.abs(n[1]) + jnp.abs(n[2]))
            u, v, w = both[6:]
            ns = [-0.5 * shear * x for x in n]
            spread = (-0.5 * lame) * (n[0] * u + n[1] * v + n[2] * w)
            over = [-0.5 * inverse * x for x in n]
            xx, yy, zz, xy, yz, xz = both[:6]
            flux = [
                spread + (2.0 * ns[0]) * u,
                spread + (2.0 * ns[1]) * v,
                spread + (2.0 * ns[2]) * w,
                ns[0] * v + ns[1] * u,
                ns[1] * w + ns[2] * v,
                ns[0] * w + ns[2] * u,
                over[0] * xx + over[1] * xy + over[2] * xz,
                over[0] * xy + over[1] * yy + over[2] * yz,
                over[0] * xz + over[1] * yz + over[2] * zz,
            ]
            for q in range(QUANT):
                fluxes[q].append(flux[q] + half * apart[q])
        lifted = dot(
            lift_w[...], stacked([jnp.concatenate(parts, axis=0) for parts in fluxes], 96)
        )
        for q in range(QUANT):
            out_ref[q] = out_ref[q] - lifted[0:BASIS, q * ELEMS : (q + 1) * ELEMS]
        for copy in copies:
            copy.wait_send()


def solution(mesh):
    rows, cols = mesh.shape["prow"], mesh.shape["pcol"]

    def per_device(*args):
        args = list(args)
        args[7] = args[7].reshape(1, ELEMS)
        vmem = pl.BlockSpec(memory_space=pltpu.VMEM)
        return pl.pallas_call(
            functools.partial(kernel, rows, cols),
            out_shape=jax.ShapeDtypeStruct((QUANT, BASIS, ELEMS), F32),
            in_specs=[vmem] * 15,
            out_specs=vmem,
            scratch_shapes=[
                pltpu.VMEM((176, 384), F32),
                pltpu.VMEM((176, 3 * KBLOCK), BF16),
                pltpu.VMEM((176, 3 * KBLOCK), BF16),
                pltpu.VMEM((96, 3 * KBLOCK), BF16),
                pltpu.VMEM((64, 288), BF16),
                pltpu.VMEM((80, 80), BF16),
                pltpu.VMEM((FACES, FACES), BF16),
                pltpu.VMEM((8 * SLOTS, FACES), BF16),
                pltpu.VMEM((8 * SLOTS, FACES), BF16),
                pltpu.VMEM((STEPS, 8, SLOTS, WIDE), F32),
                pltpu.VMEM((STEPS, 8, SLOTS, WIDE), F32),
                pltpu.SemaphoreType.DMA((STEPS, 8)),
                pltpu.SemaphoreType.DMA((STEPS, 8)),
            ],
            compiler_params=pltpu.CompilerParams(
                collective_id=0, has_side_effects=True, vmem_limit_bytes=40 * 1024 * 1024
            ),
        )(*args)

    both = ("prow", "pcol")
    return jax.shard_map(
        per_device,
        mesh=mesh,
        in_specs=(
            P(None, None, both),
            P(),
            P(),
            P(),
            P(),
            P(),
            P(),
            P(both),
            P(None, None, both),
            P(None, None, both),
            P(None, both),
            P(None, both),
            P(None, both),
            P("prow", "pcol", None, None),
            P("prow", "pcol", None, None),
        ),
        out_specs=P(None, None, both),
        check_vma=False,
    )
```

```python
import functools

import jax
import jax.numpy as jnp
from jax import lax
from jax.experimental import pallas as pl
from jax.experimental.pallas import tpu as pltpu
from jax.sharding import PartitionSpec as P

ORDER = 6
STEPS = 2
TIME_STEP = 0.8
OFFSETS = ((-1, -1), (-1, 0), (-1, 1), (0, -1), (0, 1), (1, -1), (1, 0), (1, 1))
MESH = pl.DeviceIdType.MESH
F32 = jnp.float32
BF16 = jnp.bfloat16
QUANT = 9
BASIS = 56
KBLOCK = 64
FACE = 21
FROWS = 24
ELEMS = 128
FACES = 4 * ELEMS
SLOTS = 24
WIDE = 256


def dot(a, b):
    return lax.dot_general(a, b, (((1,), (0,)), ((), ())), preferred_element_type=F32)


def dot_nt(a, b):
    return lax.dot_general(a, b, (((1,), (1,)), ((), ())), preferred_element_type=F32)


def low_of(x):
    return x - x.astype(BF16).astype(F32)


def widen(x, rows):
    if x.shape[0] == rows:
        return x
    return jnp.concatenate([x, jnp.zeros((rows - x.shape[0], x.shape[1]), F32)], axis=0)


def stacked(slabs, rows):
    columns = []
    for slab in slabs:
        full = widen(slab, rows)
        high = full.astype(BF16)
        low = (full - high.astype(F32)).astype(BF16)
        columns.append(jnp.concatenate([high, high, low], axis=0))
    return jnp.concatenate(columns, axis=1)


def stress_rates(ux, vy, wz, uv, vw, uw, lame, shear2, shear):
    spread = lame * (ux + vy + wz)
    return [
        spread + shear2 * ux,
        spread + shear2 * vy,
        spread + shear2 * wz,
        shear * uv,
        shear * vw,
        shear * uw,
    ]


def kernel(
    rows,
    cols,
    dof_hbm,
    grad_hbm,
    stiff_hbm,
    proj_hbm,
    lift_hbm,
    rot_hbm,
    mat_hbm,
    mid_hbm,
    jac_hbm,
    nrm_hbm,
    ori_hbm,
    near_hbm,
    near_face_hbm,
    send_list_hbm,
    recv_list_hbm,
    out_ref,
    dof_ref,
    grad_ref,
    stiff_ref,
    proj_ref,
    lift_ref,
    rot_ref,
    mat_ref,
    mid_ref,
    jac_ref,
    nrm_ref,
    ori_ref,
    near_ref,
    near_face_ref,
    send_list_ref,
    recv_list_ref,
    load_sem,
    tmp,
    grad_w,
    stiff_w,
    proj_w,
    lift_w,
    rot_w,
    near_w,
    give_w,
    take_w,
    send_buf,
    recv_buf,
    send_sem,
    recv_sem,
):
    loads = []
    for at, (source, dest) in enumerate(
        [
            (grad_hbm, grad_ref),
            (dof_hbm, dof_ref),
            (jac_hbm, jac_ref),
            (mat_hbm, mat_ref),
            (mid_hbm, mid_ref),
            (proj_hbm, proj_ref),
            (send_list_hbm, send_list_ref),
            (stiff_hbm, stiff_ref),
            (lift_hbm, lift_ref),
            (rot_hbm, rot_ref),
            (nrm_hbm, nrm_ref),
            (ori_hbm, ori_ref),
            (near_hbm, near_ref),
            (near_face_hbm, near_face_ref),
            (recv_list_hbm, recv_list_ref),
        ]
    ):
        load = pltpu.make_async_copy(source, dest, load_sem.at[at])
        load.start()
        loads.append(load)

    row = lax.axis_index("prow")
    col = lax.axis_index("pcol")
    partners = []
    exists = []
    for dr, dc in OFFSETS:
        there = [row + dr, col + dc]
        inside = []
        if dr:
            inside.append(there[0] >= 0 if dr < 0 else there[0] < rows)
        if dc:
            inside.append(there[1] >= 0 if dc < 0 else there[1] < cols)
        partners.append((there[0], there[1]))
        exists.append(functools.reduce(jnp.logical_and, inside))
    up_down = (row > 0).astype(jnp.int32) + (row < rows - 1).astype(jnp.int32)
    left_right = (col > 0).astype(jnp.int32) + (col < cols - 1).astype(jnp.int32)
    peers = up_down + left_right + up_down * left_right
    barrier = pltpu.get_barrier_semaphore()
    for d in range(8):

        @pl.when(exists[d])
        def _(d=d):
            pl.semaphore_signal(barrier, inc=1, device_id=partners[d], device_id_type=MESH)

        @pl.when(jnp.logical_not(exists[d]))
        def _(d=d):
            for step in range(STEPS):
                recv_buf[step, d] = jnp.zeros((SLOTS, WIDE), F32)

    tmp[...] = jnp.zeros_like(tmp)
    for load in loads:
        load.wait()

    def split_store(dest, at, block, step_k, first=True):
        height, width = block.shape
        dest[at : at + height, 0:width] = block
        dest[at : at + height, step_k : step_k + width] = low_of(block)
        dest[at : at + height, 2 * step_k : 2 * step_k + width] = block

    for d in range(3):
        split_store(tmp, d * BASIS, grad_ref[d], KBLOCK)
    grad_w[...] = tmp[0:176, 0 : 3 * KBLOCK].astype(BF16)
    for d in range(3):
        split_store(tmp, d * BASIS, stiff_ref[d], KBLOCK)
    stiff_w[...] = tmp[0:176, 0 : 3 * KBLOCK].astype(BF16)
    tmp[...] = jnp.zeros_like(tmp)
    for f in range(4):
        for i in range(FACE):
            tmp[f * FROWS + i : f * FROWS + i + 1, 0:BASIS] = proj_ref[i, f : f + 1, :]
    split_store(tmp, 0, tmp[0:96, 0:KBLOCK], KBLOCK)
    proj_w[...] = tmp[0:96, 0 : 3 * KBLOCK].astype(BF16)
    tmp[...] = jnp.zeros_like(tmp)
    for h in range(3):
        split_store(tmp, h * FROWS, rot_ref[h], FROWS)
    rot_w[...] = tmp[0:80, 0:80].astype(BF16)
    tmp[...] = jnp.zeros_like(tmp)
    for f in range(4):
        for i in range(FACE):
            tmp[f * FROWS + i : f * FROWS + i + 1, 0:BASIS] = lift_ref[i, f : f + 1, :]
    high = tmp[0:96, 0:BASIS]
    lift_w[...] = jnp.transpose(jnp.concatenate([high, low_of(high), high], axis=0)).astype(BF16)

    face_rows = lax.broadcasted_iota(jnp.int32, (FACES, ELEMS), 0)
    for f in range(4):
        near = near_ref[f : f + 1, :]
        source = jnp.where(near >= 0, near_face_ref[f : f + 1, :] * ELEMS + near, -1)
        near_w[:, f * ELEMS : (f + 1) * ELEMS] = (face_rows == source).astype(F32).astype(BF16)
    outside = jnp.concatenate([near_ref[f : f + 1, :] < 0 for f in range(4)], axis=1)
    face_ids = lax.broadcasted_iota(jnp.int32, (SLOTS, FACES), 1)
    give_ids = jnp.transpose(send_list_ref[0, 0])
    take_ids = jnp.transpose(recv_list_ref[0, 0])
    give_parts = []
    take_parts = []
    for d in range(8):
        give_parts.append((give_ids[:, d : d + 1] == face_ids).astype(F32))
        take_parts.append(
            jnp.where((take_ids[:, d : d + 1] == face_ids) & outside, 1.0, 0.0).astype(F32)
        )
    give_w[...] = jnp.concatenate(give_parts, axis=0).astype(BF16)
    take_w[...] = jnp.concatenate(take_parts, axis=0).astype(BF16)

    hot = lax.broadcasted_iota(jnp.int32, (16, ELEMS), 0) == mid_ref[...]
    table = jnp.transpose(mat_ref[...])
    density, lame, shear = [
        jnp.sum(jnp.where(hot, table[:, j : j + 1], 0.0), axis=0, keepdims=True) for j in range(3)
    ]
    inverse = 1.0 / density
    jac = [[jac_ref[d, k : k + 1, :] for k in range(3)] for d in range(3)]
    root = jnp.sqrt((lame + 2.0 * shear) * inverse)
    orient = jnp.concatenate([ori_ref[f : f + 1, :] for f in range(4)], axis=1)

    def along(slopes, columns):
        def one(place, k):
            parts = [
                jac[d][k]
                * slopes[d * BASIS : (d + 1) * BASIS, place * ELEMS : (place + 1) * ELEMS]
                for d in range(3)
            ]
            return parts[0] + parts[1] + parts[2]

        return one

    def stress_from(slopes, scale):
        one = along(slopes, 3)
        ux, vy, wz = one(0, 0), one(1, 1), one(2, 2)
        uv = one(1, 0) + one(0, 1)
        vw = one(2, 1) + one(1, 2)
        uw = one(2, 0) + one(0, 2)
        return stress_rates(
            ux, vy, wz, uv, vw, uw, scale * lame, (2.0 * scale) * shear, scale * shear
        )

    def speed_from(slopes, scale):
        one = along(slopes, 6)
        over = scale * inverse
        return [
            over * (one(0, 0) + one(3, 1) + one(5, 2)),
            over * (one(3, 0) + one(1, 1) + one(4, 2)),
            over * (one(5, 0) + one(4, 1) + one(2, 2)),
        ]

    for step in range(STEPS):
        current = dof_ref if step == 0 else out_ref
        level = [TIME_STEP * current[q] for q in range(QUANT)]
        total = list(level)
        for power in range(1, ORDER):
            scale = TIME_STEP / (power + 1)
            from_stress = dot(grad_w[...], stacked(level[:6], KBLOCK))
            from_speed = dot(grad_w[...], stacked(level[6:], KBLOCK))
            level = stress_from(from_speed, scale) + speed_from(from_stress, scale)
            total = [t + x for t, x in zip(total, level)]

        whole = stacked(total, KBLOCK)
        own = dot(proj_w[...], whole)
        faces = jnp.concatenate(
            [
                jnp.concatenate(
                    [
                        own[f * FROWS : (f + 1) * FROWS, q * ELEMS : (q + 1) * ELEMS]
                        for f in range(4)
                    ],
                    axis=1,
                )
                for q in range(QUANT)
            ]
            + [jnp.zeros((WIDE - QUANT * FROWS, FACES), F32)],
            axis=0,
        )
        faces_high = faces.astype(BF16)
        faces_low = (faces - faces_high.astype(F32)).astype(BF16)
        outgoing = dot_nt(give_w[...], faces_high) + dot_nt(give_w[...], faces_low)
        for d in range(8):
            send_buf[step, d] = outgoing[d * SLOTS : (d + 1) * SLOTS]
        if step == 0:
            pl.semaphore_wait(barrier, peers)
        copies = []
        for d in range(8):
            copy = pltpu.make_async_remote_copy(
                src_ref=send_buf.at[step, d],
                dst_ref=recv_buf.at[step, 7 - d],
                send_sem=send_sem.at[step, d],
                recv_sem=recv_sem.at[step, 7 - d],
                device_id=partners[d],
                device_id_type=MESH,
            )
            copies.append(copy)
            pl.when(exists[d])(copy.start)

        slopes = dot(stiff_w[...], whole)
        volume = stress_from(slopes[:, 6 * ELEMS :], -1.0) + speed_from(slopes[:, : 6 * ELEMS], -1.0)
        for q in range(QUANT):
            out_ref[q] = current[q] + volume[q]
        beside = dot(faces_high, near_w[...]) + dot(faces_low, near_w[...])

        for d in range(8):
            pl.when(exists[7 - d])(copies[d].wait_recv)
        got = jnp.transpose(
            jnp.concatenate([recv_buf[step, d] for d in range(8)], axis=0)
        )
        got_high = got.astype(BF16)
        got_low = (got - got_high.astype(F32)).astype(BF16)
        beside = beside + dot(got_high, take_w[...]) + dot(got_low, take_w[...])

        turned = []
        for q in range(QUANT):
            block = beside[q * FROWS : (q + 1) * FROWS]
            low = low_of(block)
            right = jnp.concatenate([block, block, low, jnp.zeros((8, FACES), F32)], axis=0)
            each = dot(rot_w[...], right.astype(BF16))
            turned.append(
                jnp.where(
                    orient == 0,
                    each[0:FROWS],
                    jnp.where(orient == 1, each[FROWS : 2 * FROWS], each[2 * FROWS : 3 * FROWS]),
                )
            )

        fluxes = [[] for _ in range(QUANT)]
        for f in range(4):
            here = slice(f * ELEMS, (f + 1) * ELEMS)
            n = [nrm_ref[k, f : f + 1, :] for k in range(3)]
            both = []
            apart = []
            for q in range(QUANT):
                mine = own[f * FROWS : (f + 1) * FROWS, q * ELEMS : (q + 1) * ELEMS]
                theirs = turned[q][:, here]
                both.append(mine + theirs)
                apart.append(mine - theirs)
            half = 0.5 * root * (jnp.abs(n[0]) + jnp.abs(n[1]) + jnp.abs(n[2]))
            u, v, w = both[6:]
            ns = [-0.5 * shear * x for x in n]
            spread = (-0.5 * lame) * (n[0] * u + n[1] * v + n[2] * w)
            over = [-0.5 * inverse * x for x in n]
            xx, yy, zz, xy, yz, xz = both[:6]
            flux = [
                spread + (2.0 * ns[0]) * u,
                spread + (2.0 * ns[1]) * v,
                spread + (2.0 * ns[2]) * w,
                ns[0] * v + ns[1] * u,
                ns[1] * w + ns[2] * v,
                ns[0] * w + ns[2] * u,
                over[0] * xx + over[1] * xy + over[2] * xz,
                over[0] * xy + over[1] * yy + over[2] * yz,
                over[0] * xz + over[1] * yz + over[2] * zz,
            ]
            for q in range(QUANT):
                fluxes[q].append(flux[q] + half * apart[q])
        lifted = dot(
            lift_w[...], stacked([jnp.concatenate(parts, axis=0) for parts in fluxes], 96)
        )
        for q in range(QUANT):
            out_ref[q] = out_ref[q] - lifted[:, q * ELEMS : (q + 1) * ELEMS]
        for d in range(8):
            pl.when(exists[d])(copies[d].wait_send)


def solution(mesh):
    rows, cols = mesh.shape["prow"], mesh.shape["pcol"]

    def per_device(*args):
        args = list(args)
        args[3] = args[3].transpose(1, 0, 2)
        args[4] = args[4].transpose(2, 0, 1)
        args[6] = args[6].transpose(1, 0)
        args[7] = args[7].reshape(1, ELEMS)
        args[9] = args[9].transpose(1, 0, 2)
        vmem = pl.BlockSpec(memory_space=pltpu.VMEM)
        return pl.pallas_call(
            functools.partial(kernel, rows, cols),
            out_shape=jax.ShapeDtypeStruct((QUANT, BASIS, ELEMS), F32),
            in_specs=[pl.BlockSpec(memory_space=pltpu.HBM)] * 15,
            out_specs=vmem,
            scratch_shapes=[pltpu.VMEM(x.shape, x.dtype) for x in args]
            + [
                pltpu.SemaphoreType.DMA((15,)),
                pltpu.VMEM((176, 384), F32),
                pltpu.VMEM((176, 3 * KBLOCK), BF16),
                pltpu.VMEM((176, 3 * KBLOCK), BF16),
                pltpu.VMEM((96, 3 * KBLOCK), BF16),
                pltpu.VMEM((BASIS, 288), BF16),
                pltpu.VMEM((80, 80), BF16),
                pltpu.VMEM((FACES, FACES), BF16),
                pltpu.VMEM((8 * SLOTS, FACES), BF16),
                pltpu.VMEM((8 * SLOTS, FACES), BF16),
                pltpu.VMEM((STEPS, 8, SLOTS, WIDE), F32),
                pltpu.VMEM((STEPS, 8, SLOTS, WIDE), F32),
                pltpu.SemaphoreType.DMA((STEPS, 8)),
                pltpu.SemaphoreType.DMA((STEPS, 8)),
            ],
            compiler_params=pltpu.CompilerParams(
                collective_id=0, has_side_effects=True, vmem_limit_bytes=63 * 1024 * 1024
            ),
        )(*args)

    both = ("prow", "pcol")
    return jax.shard_map(
        per_device,
        mesh=mesh,
        in_specs=(
            P(None, None, both),
            P(),
            P(),
            P(),
            P(),
            P(),
            P(),
            P(both),
            P(None, None, both),
            P(None, None, both),
            P(None, both),
            P(None, both),
            P(None, both),
            P("prow", "pcol", None, None),
            P("prow", "pcol", None, None),
        ),
        out_specs=P(None, None, both),
        check_vma=False,
    )
```

```python
import functools

import jax
import jax.numpy as jnp
from jax import lax
from jax.experimental import pallas as pl
from jax.experimental.pallas import tpu as pltpu
from jax.sharding import PartitionSpec as P

ORDER = 6
STEPS = 2
TIME_STEP = 0.8
OFFSETS = ((-1, -1), (-1, 0), (-1, 1), (0, -1), (0, 1), (1, -1), (1, 0), (1, 1))
FAR_FIRST = (0, 2, 5, 7, 3, 4, 1, 6)
MESH = pl.DeviceIdType.MESH
F32 = jnp.float32
BF16 = jnp.bfloat16
QUANT = 9
BASIS = 56
KBLOCK = 64
FACE = 21
FROWS = 24
ELEMS = 128
FACES = 4 * ELEMS
SLOTS = 24
WIDE = 256


(
    GRAD,
    DOF,
    JAC,
    MAT,
    MID,
    PROJ,
    SEND_LIST,
    STIFF,
    LIFT,
    ROT,
    NRM,
    ORI,
    NEAR,
    NEAR_FACE,
    RECV_LIST,
) = range(15)


def dot(a, b):
    return lax.dot_general(a, b, (((1,), (0,)), ((), ())), preferred_element_type=F32)


def dot_nt(a, b):
    return lax.dot_general(a, b, (((1,), (1,)), ((), ())), preferred_element_type=F32)


def low_of(x):
    return x - x.astype(BF16).astype(F32)


def widen(x, rows):
    if x.shape[0] == rows:
        return x
    return jnp.concatenate([x, jnp.zeros((rows - x.shape[0], x.shape[1]), F32)], axis=0)


def stacked(slabs, rows):
    columns = []
    for slab in slabs:
        full = widen(slab, rows)
        high = full.astype(BF16)
        low = (full - high.astype(F32)).astype(BF16)
        columns.append(jnp.concatenate([high, high, low], axis=0))
    return jnp.concatenate(columns, axis=1)


def stress_rates(ux, vy, wz, uv, vw, uw, lame, shear2, shear):
    spread = lame * (ux + vy + wz)
    return [
        spread + shear2 * ux,
        spread + shear2 * vy,
        spread + shear2 * wz,
        shear * uv,
        shear * vw,
        shear * uw,
    ]


def kernel(
    rows,
    cols,
    dof_hbm,
    grad_hbm,
    stiff_hbm,
    proj_hbm,
    lift_hbm,
    rot_hbm,
    mat_hbm,
    mid_hbm,
    jac_hbm,
    nrm_hbm,
    ori_hbm,
    near_hbm,
    near_face_hbm,
    send_list_hbm,
    recv_list_hbm,
    out_ref,
    dof_ref,
    grad_ref,
    stiff_ref,
    proj_ref,
    lift_ref,
    rot_ref,
    mat_ref,
    mid_ref,
    jac_ref,
    nrm_ref,
    ori_ref,
    near_ref,
    near_face_ref,
    send_list_ref,
    recv_list_ref,
    load_sem,
    tmp,
    grad_w,
    stiff_w,
    proj_w,
    lift_w,
    rot_w,
    near_w,
    give_w,
    take_w,
    send_buf,
    recv_buf,
    send_sem,
    recv_sem,
):
    loads = []
    for at, (source, dest) in enumerate(
        [
            (grad_hbm, grad_ref),
            (dof_hbm, dof_ref),
            (jac_hbm, jac_ref),
            (mat_hbm, mat_ref),
            (mid_hbm, mid_ref),
            (proj_hbm, proj_ref),
            (send_list_hbm, send_list_ref),
            (stiff_hbm, stiff_ref),
            (lift_hbm, lift_ref),
            (rot_hbm, rot_ref),
            (nrm_hbm, nrm_ref),
            (ori_hbm, ori_ref),
            (near_hbm, near_ref),
            (near_face_hbm, near_face_ref),
            (recv_list_hbm, recv_list_ref),
        ]
    ):
        load = pltpu.make_async_copy(source, dest, load_sem.at[at])
        load.start()
        loads.append(load)

    row = lax.axis_index("prow")
    col = lax.axis_index("pcol")
    partners = []
    exists = []
    for dr, dc in OFFSETS:
        there = [row + dr, col + dc]
        inside = []
        if dr:
            inside.append(there[0] >= 0 if dr < 0 else there[0] < rows)
        if dc:
            inside.append(there[1] >= 0 if dc < 0 else there[1] < cols)
        partners.append((there[0], there[1]))
        exists.append(functools.reduce(jnp.logical_and, inside))
    up_down = (row > 0).astype(jnp.int32) + (row < rows - 1).astype(jnp.int32)
    left_right = (col > 0).astype(jnp.int32) + (col < cols - 1).astype(jnp.int32)
    peers = up_down + left_right + up_down * left_right
    barrier = pltpu.get_barrier_semaphore()
    for d in range(8):

        @pl.when(exists[d])
        def _(d=d):
            pl.semaphore_signal(barrier, inc=1, device_id=partners[d], device_id_type=MESH)

        @pl.when(jnp.logical_not(exists[d]))
        def _(d=d):
            for step in range(STEPS):
                recv_buf[step, d] = jnp.zeros((SLOTS, WIDE), F32)

    def arrived(*names):
        for name in names:
            loads[name].wait()

    def split_store(at, block, step_k):
        height, width = block.shape
        low = low_of(block)
        tmp[at : at + height, 0:width] = block
        tmp[at : at + height, step_k : step_k + width] = low
        tmp[at : at + height, 2 * step_k : 2 * step_k + width] = block

    def derivative_matrix(source, dest):
        for block in range(7):
            for d in range(3):
                split_store(block * 24 + d * 8, source[d, block * 8 : block * 8 + 8], KBLOCK)
        dest[...] = tmp[0:176, 0 : 3 * KBLOCK].astype(BF16)

    def face_matrix(source):
        for f in range(4):
            for i in range(FACE):
                tmp[f * FROWS + i : f * FROWS + i + 1, 0:BASIS] = source[i, f : f + 1, :]

    def one_hot(ids_ref, dest, keep):
        ids = jnp.transpose(ids_ref[0, 0])
        face_ids = lax.broadcasted_iota(jnp.int32, (SLOTS, FACES), 1)
        parts = []
        for d in range(8):
            hit = ids[:, d : d + 1] == face_ids
            if keep is not None:
                hit = hit & keep
            parts.append(jnp.where(hit, 1.0, 0.0).astype(F32))
        dest[...] = jnp.concatenate(parts, axis=0).astype(BF16)

    tmp[...] = jnp.zeros_like(tmp)
    arrived(GRAD)
    derivative_matrix(grad_ref, grad_w)

    arrived(JAC, MAT, MID)
    hot = lax.broadcasted_iota(jnp.int32, (16, ELEMS), 0) == mid_ref[...]
    table = jnp.transpose(mat_ref[...])
    density, lame, shear = [
        jnp.sum(jnp.where(hot, table[:, j : j + 1], 0.0), axis=0, keepdims=True) for j in range(3)
    ]
    inverse = 1.0 / density
    lame8, shear8, inverse8 = [
        jnp.broadcast_to(x, (8, ELEMS)) for x in (lame, shear, inverse)
    ]
    jac = [
        [jnp.broadcast_to(jac_ref[d, k : k + 1, :], (8, ELEMS)) for k in range(3)]
        for d in range(3)
    ]
    arrived(DOF)
    root = jnp.sqrt((lame + 2.0 * shear) * inverse)

    def along(slopes, block):
        def one(place, k):
            parts = [
                jac[d][k]
                * slopes[
                    block * 24 + d * 8 : block * 24 + d * 8 + 8,
                    place * ELEMS : (place + 1) * ELEMS,
                ]
                for d in range(3)
            ]
            return parts[0] + parts[1] + parts[2]

        return one

    def by_blocks(rates):
        return [jnp.concatenate(list(x), axis=0) for x in zip(*[rates(b) for b in range(7)])]

    def stress_from(slopes, scale):
        lame_s, shear2_s, shear_s = scale * lame8, (2.0 * scale) * shear8, scale * shear8

        def rates(block):
            one = along(slopes, block)
            ux, vy, wz = one(0, 0), one(1, 1), one(2, 2)
            uv = one(1, 0) + one(0, 1)
            vw = one(2, 1) + one(1, 2)
            uw = one(2, 0) + one(0, 2)
            return stress_rates(ux, vy, wz, uv, vw, uw, lame_s, shear2_s, shear_s)

        return by_blocks(rates)

    def speed_from(slopes, scale):
        over = scale * inverse8

        def rates(block):
            one = along(slopes, block)
            return [
                over * (one(0, 0) + one(3, 1) + one(5, 2)),
                over * (one(3, 0) + one(1, 1) + one(4, 2)),
                over * (one(5, 0) + one(4, 1) + one(2, 2)),
            ]

        return by_blocks(rates)

    for step in range(STEPS):
        current = dof_ref if step == 0 else out_ref
        level = [TIME_STEP * current[q] for q in range(QUANT)]
        total = list(level)
        of_speed = dot(grad_w[...], stacked(level[6:], KBLOCK))
        of_stress = dot(grad_w[...], stacked(level[:6], KBLOCK))
        for power in range(1, ORDER):
            scale = TIME_STEP / (power + 1)
            stress = stress_from(of_speed, scale)
            if power < ORDER - 1:
                next_of_stress = dot(grad_w[...], stacked(stress, KBLOCK))
            speed = speed_from(of_stress, scale)
            if power < ORDER - 1:
                of_speed = dot(grad_w[...], stacked(speed, KBLOCK))
                of_stress = next_of_stress
            total = [t + x for t, x in zip(total, stress + speed)]

        if step == 0:
            arrived(PROJ, SEND_LIST)
            tmp[...] = jnp.zeros_like(tmp)
            face_matrix(proj_ref)
            split_store(0, tmp[0:96, 0:KBLOCK], KBLOCK)
            proj_w[...] = tmp[0:96, 0 : 3 * KBLOCK].astype(BF16)
            one_hot(send_list_ref, give_w, None)
        whole = stacked(total, KBLOCK)
        own = dot(proj_w[...], whole)
        faces = jnp.concatenate(
            [
                jnp.concatenate(
                    [
                        own[f * FROWS : (f + 1) * FROWS, q * ELEMS : (q + 1) * ELEMS]
                        for f in range(4)
                    ],
                    axis=1,
                )
                for q in range(QUANT)
            ]
            + [jnp.zeros((WIDE - QUANT * FROWS, FACES), F32)],
            axis=0,
        )
        faces_high = faces.astype(BF16)
        faces_low = (faces - faces_high.astype(F32)).astype(BF16)
        outgoing = dot_nt(give_w[...], faces_high) + dot_nt(give_w[...], faces_low)
        for d in range(8):
            send_buf[step, d] = outgoing[d * SLOTS : (d + 1) * SLOTS]
        if step == 0:
            pl.semaphore_wait(barrier, peers)
        copies = [None] * 8
        for d in FAR_FIRST:
            copy = pltpu.make_async_remote_copy(
                src_ref=send_buf.at[step, d],
                dst_ref=recv_buf.at[step, 7 - d],
                send_sem=send_sem.at[step, d],
                recv_sem=recv_sem.at[step, 7 - d],
                device_id=partners[d],
                device_id_type=MESH,
            )
            copies[d] = copy
            pl.when(exists[d])(copy.start)

        if step == 0:
            arrived(STIFF, LIFT, ROT, NRM, ORI, NEAR, NEAR_FACE, RECV_LIST)
            derivative_matrix(stiff_ref, stiff_w)
            tmp[...] = jnp.zeros_like(tmp)
            for h in range(3):
                split_store(h * FROWS, rot_ref[h], FROWS)
            rot_w[...] = tmp[0:80, 0:80].astype(BF16)
            tmp[...] = jnp.zeros_like(tmp)
            face_matrix(lift_ref)
            high = tmp[0:96, 0:BASIS]
            lift_w[...] = jnp.transpose(
                jnp.concatenate([high, low_of(high), high], axis=0)
            ).astype(BF16)
            face_rows = lax.broadcasted_iota(jnp.int32, (FACES, ELEMS), 0)
            for f in range(4):
                near = near_ref[f : f + 1, :]
                source = jnp.where(near >= 0, near_face_ref[f : f + 1, :] * ELEMS + near, -1)
                near_w[:, f * ELEMS : (f + 1) * ELEMS] = (
                    (face_rows == source).astype(F32).astype(BF16)
                )
            outside = jnp.concatenate([near_ref[f : f + 1, :] < 0 for f in range(4)], axis=1)
            one_hot(recv_list_ref, take_w, outside)
        orient = jnp.concatenate([ori_ref[f : f + 1, :] for f in range(4)], axis=1)
        slopes = dot(stiff_w[...], whole)
        volume = stress_from(slopes[:, 6 * ELEMS :], -1.0) + speed_from(slopes[:, : 6 * ELEMS], -1.0)
        for q in range(QUANT):
            out_ref[q] = current[q] + volume[q]
        beside = dot(faces_high, near_w[...]) + dot(faces_low, near_w[...])

        for d in range(8):
            pl.when(exists[7 - d])(copies[d].wait_recv)
        got = jnp.transpose(
            jnp.concatenate([recv_buf[step, d] for d in range(8)], axis=0)
        )
        got_high = got.astype(BF16)
        got_low = (got - got_high.astype(F32)).astype(BF16)
        beside = beside + dot(got_high, take_w[...]) + dot(got_low, take_w[...])

        turned = []
        for q in range(QUANT):
            block = beside[q * FROWS : (q + 1) * FROWS]
            low = low_of(block)
            right = jnp.concatenate([block, block, low, jnp.zeros((8, FACES), F32)], axis=0)
            each = dot(rot_w[...], right.astype(BF16))
            turned.append(
                jnp.where(
                    orient == 0,
                    each[0:FROWS],
                    jnp.where(orient == 1, each[FROWS : 2 * FROWS], each[2 * FROWS : 3 * FROWS]),
                )
            )

        fluxes = [[] for _ in range(QUANT)]
        for f in range(4):
            here = slice(f * ELEMS, (f + 1) * ELEMS)
            n = [nrm_ref[k, f : f + 1, :] for k in range(3)]
            both = []
            apart = []
            for q in range(QUANT):
                mine = own[f * FROWS : (f + 1) * FROWS, q * ELEMS : (q + 1) * ELEMS]
                theirs = turned[q][:, here]
                both.append(mine + theirs)
                apart.append(mine - theirs)
            half = 0.5 * root * (jnp.abs(n[0]) + jnp.abs(n[1]) + jnp.abs(n[2]))
            u, v, w = both[6:]
            ns = [-0.5 * shear * x for x in n]
            spread = (-0.5 * lame) * (n[0] * u + n[1] * v + n[2] * w)
            over = [-0.5 * inverse * x for x in n]
            xx, yy, zz, xy, yz, xz = both[:6]
            flux = [
                spread + (2.0 * ns[0]) * u,
                spread + (2.0 * ns[1]) * v,
                spread + (2.0 * ns[2]) * w,
                ns[0] * v + ns[1] * u,
                ns[1] * w + ns[2] * v,
                ns[0] * w + ns[2] * u,
                over[0] * xx + over[1] * xy + over[2] * xz,
                over[0] * xy + over[1] * yy + over[2] * yz,
                over[0] * xz + over[1] * yz + over[2] * zz,
            ]
            for q in range(QUANT):
                fluxes[q].append(flux[q] + half * apart[q])
        lifted = dot(
            lift_w[...], stacked([jnp.concatenate(parts, axis=0) for parts in fluxes], 96)
        )
        for q in range(QUANT):
            out_ref[q] = out_ref[q] - lifted[:, q * ELEMS : (q + 1) * ELEMS]
        for d in range(8):
            pl.when(exists[d])(copies[d].wait_send)


def solution(mesh):
    rows, cols = mesh.shape["prow"], mesh.shape["pcol"]

    def per_device(*args):
        args = list(args)
        args[3] = args[3].transpose(1, 0, 2)
        args[4] = args[4].transpose(2, 0, 1)
        args[6] = args[6].transpose(1, 0)
        args[7] = args[7].reshape(1, ELEMS)
        args[9] = args[9].transpose(1, 0, 2)
        vmem = pl.BlockSpec(memory_space=pltpu.VMEM)
        return pl.pallas_call(
            functools.partial(kernel, rows, cols),
            out_shape=pltpu.VMEM((QUANT, BASIS, ELEMS), F32),
            in_specs=[pl.BlockSpec(memory_space=pltpu.HBM)] * 15,
            out_specs=vmem,
            scratch_shapes=[pltpu.VMEM(x.shape, x.dtype) for x in args]
            + [
                pltpu.SemaphoreType.DMA((15,)),
                pltpu.VMEM((176, 384), F32),
                pltpu.VMEM((176, 3 * KBLOCK), BF16),
                pltpu.VMEM((176, 3 * KBLOCK), BF16),
                pltpu.VMEM((96, 3 * KBLOCK), BF16),
                pltpu.VMEM((BASIS, 288), BF16),
                pltpu.VMEM((80, 80), BF16),
                pltpu.VMEM((FACES, FACES), BF16),
                pltpu.VMEM((8 * SLOTS, FACES), BF16),
                pltpu.VMEM((8 * SLOTS, FACES), BF16),
                pltpu.VMEM((STEPS, 8, SLOTS, WIDE), F32),
                pltpu.VMEM((STEPS, 8, SLOTS, WIDE), F32),
                pltpu.SemaphoreType.DMA((STEPS, 8)),
                pltpu.SemaphoreType.DMA((STEPS, 8)),
            ],
            compiler_params=pltpu.CompilerParams(
                collective_id=0, has_side_effects=True, vmem_limit_bytes=40 * 1024 * 1024
            ),
        )(*[pltpu.with_memory_space_constraint(x, pltpu.HBM) for x in args])

    both = ("prow", "pcol")
    return jax.shard_map(
        per_device,
        mesh=mesh,
        in_specs=(
            P(None, None, both),
            P(),
            P(),
            P(),
            P(),
            P(),
            P(),
            P(both),
            P(None, None, both),
            P(None, None, both),
            P(None, both),
            P(None, both),
            P(None, both),
            P("prow", "pcol", None, None),
            P("prow", "pcol", None, None),
        ),
        out_specs=P(None, None, both),
        check_vma=False,
    )
```

```python
import functools

import jax
import jax.numpy as jnp
from jax import lax
from jax.experimental import pallas as pl
from jax.experimental.pallas import tpu as pltpu
from jax.sharding import PartitionSpec as P

ORDER = 6
STEPS = 2
TIME_STEP = 0.8
OFFSETS = ((-1, -1), (-1, 0), (-1, 1), (0, -1), (0, 1), (1, -1), (1, 0), (1, 1))
FAR_FIRST = (0, 2, 5, 7, 3, 4, 1, 6)
MESH = pl.DeviceIdType.MESH
F32 = jnp.float32
BF16 = jnp.bfloat16
QUANT = 9
BASIS = 56
KBLOCK = 64
FACE = 21
FROWS = 24
ELEMS = 128
FACES = 4 * ELEMS
SLOTS = 24
FIRST = 128
REST = 64
HALF = 12
HROWS = 16


(
    GRAD,
    DOF,
    JAC,
    MAT,
    MID,
    PROJ,
    SEND_LIST,
    STIFF,
    LIFT,
    ROT,
    NRM,
    ORI,
    NEAR,
    NEAR_FACE,
    RECV_LIST,
) = range(15)


def dot(a, b):
    return lax.dot_general(a, b, (((1,), (0,)), ((), ())), preferred_element_type=F32)


def dot_nt(a, b):
    return lax.dot_general(a, b, (((1,), (1,)), ((), ())), preferred_element_type=F32)


def low_of(x):
    return x - x.astype(BF16).astype(F32)


def widen(x, rows):
    if x.shape[0] == rows:
        return x
    return jnp.concatenate([x, jnp.zeros((rows - x.shape[0], x.shape[1]), F32)], axis=0)


def stacked(slabs, rows):
    columns = []
    for slab in slabs:
        full = widen(slab, rows)
        high = full.astype(BF16)
        low = (full - high.astype(F32)).astype(BF16)
        columns.append(jnp.concatenate([high, high, low], axis=0))
    return jnp.concatenate(columns, axis=1)


def stress_rates(ux, vy, wz, uv, vw, uw, lame, shear2, shear):
    spread = lame * (ux + vy + wz)
    return [
        spread + shear2 * ux,
        spread + shear2 * vy,
        spread + shear2 * wz,
        shear * uv,
        shear * vw,
        shear * uw,
    ]


def kernel(
    rows,
    cols,
    dof_hbm,
    grad_hbm,
    stiff_hbm,
    proj_hbm,
    lift_hbm,
    rot_hbm,
    mat_hbm,
    mid_hbm,
    jac_hbm,
    nrm_hbm,
    ori_hbm,
    near_hbm,
    near_face_hbm,
    send_list_hbm,
    recv_list_hbm,
    out_ref,
    dof_ref,
    grad_ref,
    stiff_ref,
    proj_ref,
    lift_ref,
    rot_ref,
    mat_ref,
    mid_ref,
    jac_ref,
    nrm_ref,
    ori_ref,
    near_ref,
    near_face_ref,
    send_list_ref,
    recv_list_ref,
    load_sem,
    tmp,
    grad_w,
    stiff_w,
    proj_w,
    last_w,
    lift_w,
    rot_w,
    rot_last_w,
    near_w,
    give_w,
    give_half_w,
    take_w,
    take_half_w,
    send_first,
    send_rest,
    recv_first,
    recv_rest,
    send_sem,
    recv_sem,
):
    loads = []
    for at, (source, dest) in enumerate(
        [
            (grad_hbm, grad_ref),
            (dof_hbm, dof_ref),
            (jac_hbm, jac_ref),
            (mat_hbm, mat_ref),
            (mid_hbm, mid_ref),
            (proj_hbm, proj_ref),
            (send_list_hbm, send_list_ref),
            (stiff_hbm, stiff_ref),
            (lift_hbm, lift_ref),
            (rot_hbm, rot_ref),
            (nrm_hbm, nrm_ref),
            (ori_hbm, ori_ref),
            (near_hbm, near_ref),
            (near_face_hbm, near_face_ref),
            (recv_list_hbm, recv_list_ref),
        ]
    ):
        load = pltpu.make_async_copy(source, dest, load_sem.at[at])
        load.start()
        loads.append(load)

    row = lax.axis_index("prow")
    col = lax.axis_index("pcol")
    partners = []
    exists = []
    for dr, dc in OFFSETS:
        there = [row + dr, col + dc]
        inside = []
        if dr:
            inside.append(there[0] >= 0 if dr < 0 else there[0] < rows)
        if dc:
            inside.append(there[1] >= 0 if dc < 0 else there[1] < cols)
        partners.append((there[0], there[1]))
        exists.append(functools.reduce(jnp.logical_and, inside))
    up_down = (row > 0).astype(jnp.int32) + (row < rows - 1).astype(jnp.int32)
    left_right = (col > 0).astype(jnp.int32) + (col < cols - 1).astype(jnp.int32)
    peers = up_down + left_right + up_down * left_right
    barrier = pltpu.get_barrier_semaphore()
    for d in range(8):

        @pl.when(exists[d])
        def _(d=d):
            pl.semaphore_signal(barrier, inc=1, device_id=partners[d], device_id_type=MESH)

        @pl.when(jnp.logical_not(exists[d]))
        def _(d=d):
            for step in range(STEPS):
                recv_first[step, d] = jnp.zeros((SLOTS, ELEMS), F32)
                recv_rest[step, d] = jnp.zeros((HROWS, ELEMS), F32)

    def arrived(*names):
        for name in names:
            loads[name].wait()

    def split_store(at, block, step_k):
        height, width = block.shape
        low = low_of(block)
        tmp[at : at + height, 0:width] = block
        tmp[at : at + height, step_k : step_k + width] = low
        tmp[at : at + height, 2 * step_k : 2 * step_k + width] = block

    def derivative_matrix(source, dest):
        for block in range(7):
            for d in range(3):
                split_store(block * 24 + d * 8, source[d, block * 8 : block * 8 + 8], KBLOCK)
        dest[...] = tmp[0:176, 0 : 3 * KBLOCK].astype(BF16)

    def face_matrix(source):
        for f in range(4):
            for i in range(FACE):
                tmp[f * FROWS + i : f * FROWS + i + 1, 0:BASIS] = source[i, f : f + 1, :]

    def one_hot(columns, dest, keep):
        parts = []
        for part in columns:
            face_ids = lax.broadcasted_iota(jnp.int32, (part.shape[0], FACES), 1)
            for d in range(8):
                hit = part[:, d : d + 1] == face_ids
                if keep is not None:
                    hit = hit & keep
                parts.append(jnp.where(hit, 1.0, 0.0).astype(F32))
        dest[...] = jnp.concatenate(parts, axis=0).astype(BF16)

    def halves(ids):
        none = jnp.full((HROWS - HALF, 8), -1, jnp.int32)
        return [jnp.concatenate([ids[at : at + HALF], none], axis=0) for at in (0, HALF)]

    tmp[...] = jnp.zeros_like(tmp)
    arrived(GRAD)
    derivative_matrix(grad_ref, grad_w)

    arrived(JAC, MAT, MID)
    hot = lax.broadcasted_iota(jnp.int32, (16, ELEMS), 0) == mid_ref[...]
    table = jnp.transpose(mat_ref[...])
    density, lame, shear = [
        jnp.sum(jnp.where(hot, table[:, j : j + 1], 0.0), axis=0, keepdims=True) for j in range(3)
    ]
    inverse = 1.0 / density
    lame8, shear8, inverse8 = [
        jnp.broadcast_to(x, (8, ELEMS)) for x in (lame, shear, inverse)
    ]
    jac = [
        [jnp.broadcast_to(jac_ref[d, k : k + 1, :], (8, ELEMS)) for k in range(3)]
        for d in range(3)
    ]
    arrived(DOF, PROJ, SEND_LIST)
    root = jnp.sqrt((lame + 2.0 * shear) * inverse)

    def along(slopes, block):
        def one(place, k):
            parts = [
                jac[d][k]
                * slopes[
                    block * 24 + d * 8 : block * 24 + d * 8 + 8,
                    place * ELEMS : (place + 1) * ELEMS,
                ]
                for d in range(3)
            ]
            return parts[0] + parts[1] + parts[2]

        return one

    def by_blocks(rates):
        return [jnp.concatenate(list(x), axis=0) for x in zip(*[rates(b) for b in range(7)])]

    def stress_from(slopes, scale):
        lame_s, shear2_s, shear_s = scale * lame8, (2.0 * scale) * shear8, scale * shear8

        def rates(block):
            one = along(slopes, block)
            ux, vy, wz = one(0, 0), one(1, 1), one(2, 2)
            uv = one(1, 0) + one(0, 1)
            vw = one(2, 1) + one(1, 2)
            uw = one(2, 0) + one(0, 2)
            return stress_rates(ux, vy, wz, uv, vw, uw, lame_s, shear2_s, shear_s)

        return by_blocks(rates)

    def speed_from(slopes, scale):
        over = scale * inverse8

        def rates(block):
            one = along(slopes, block)
            return [
                over * (one(0, 0) + one(3, 1) + one(5, 2)),
                over * (one(3, 0) + one(1, 1) + one(4, 2)),
                over * (one(5, 0) + one(4, 1) + one(2, 2)),
            ]

        return by_blocks(rates)

    for step in range(STEPS):
        current = dof_ref if step == 0 else out_ref
        level = [TIME_STEP * current[q] for q in range(QUANT)]
        total = list(level)
        of_speed = dot(grad_w[...], stacked(level[6:], KBLOCK))
        of_stress = dot(grad_w[...], stacked(level[:6], KBLOCK))
        for power in range(1, ORDER):
            scale = TIME_STEP / (power + 1)
            stress = stress_from(of_speed, scale)
            if power < ORDER - 1:
                next_of_stress = dot(grad_w[...], stacked(stress, KBLOCK))
            speed = speed_from(of_stress, scale)
            if power < ORDER - 1:
                of_speed = dot(grad_w[...], stacked(speed, KBLOCK))
                of_stress = next_of_stress
            total = [t + x for t, x in zip(total, stress + speed)]

        if step == 0:
            tmp[...] = jnp.zeros_like(tmp)
            face_matrix(proj_ref)
            split_store(0, tmp[0:96, 0:KBLOCK], KBLOCK)
            proj_w[...] = tmp[0:96, 0 : 3 * KBLOCK].astype(BF16)
            tmp[...] = jnp.zeros_like(tmp)
            for f in range(4):
                for i in range(FACE):
                    at = (f * 7 + i // 3) * 8 + 5 + i % 3
                    tmp[at : at + 1, 0:BASIS] = proj_ref[i, f : f + 1, :]
            split_store(0, tmp[0:224, 0:KBLOCK], KBLOCK)
            last_w[...] = tmp[0:224, 0 : 3 * KBLOCK].astype(BF16)
            give_ids = jnp.transpose(send_list_ref[0, 0])
            one_hot([give_ids], give_w, None)
        whole = stacked(total, KBLOCK)
        own = dot(proj_w[...], whole)
        spare = dot(last_w[...], whole[:, (QUANT - 1) * ELEMS :])
        faces = []
        for q in range(QUANT - 1):
            row_of = []
            for f in range(4):
                block = own[f * FROWS : (f + 1) * FROWS, q * ELEMS : (q + 1) * ELEMS]
                if q < 7:
                    at = (f * 7 + q) * 8
                    block = jnp.concatenate([block[0:16], block[16:24] + spare[at : at + 8]], axis=0)
                row_of.append(block)
            faces.append(jnp.concatenate(row_of, axis=1))
        faces = jnp.concatenate(faces, axis=0)
        faces_high = faces.astype(BF16)
        faces_low = (faces - faces_high.astype(F32)).astype(BF16)
        outgoing = dot_nt(give_w[...], faces_high[0:FIRST]) + dot_nt(give_w[...], faces_low[0:FIRST])
        for d in range(8):
            send_first[step, d] = outgoing[d * SLOTS : (d + 1) * SLOTS]
        if step == 0:
            pl.semaphore_wait(barrier, peers)
        copies = {}

        def send(source, dest, part):
            for d in FAR_FIRST:
                copy = pltpu.make_async_remote_copy(
                    src_ref=source.at[step, d],
                    dst_ref=dest.at[step, 7 - d],
                    send_sem=send_sem.at[step, part, d],
                    recv_sem=recv_sem.at[step, part, 7 - d],
                    device_id=partners[d],
                    device_id_type=MESH,
                )
                copies[part, d] = copy
                pl.when(exists[d])(copy.start)

        send(send_first, recv_first, 0)
        if step == 0:
            one_hot(halves(give_ids), give_half_w, None)
        outgoing = dot_nt(give_half_w[...], faces_high[FIRST:]) + dot_nt(
            give_half_w[...], faces_low[FIRST:]
        )
        outgoing = jnp.concatenate([outgoing[0:128], outgoing[128:256]], axis=1)
        for d in range(8):
            send_rest[step, d] = outgoing[d * HROWS : (d + 1) * HROWS]
        send(send_rest, recv_rest, 1)

        if step == 0:
            arrived(STIFF, LIFT, ROT, NRM, ORI, NEAR, NEAR_FACE, RECV_LIST)
            derivative_matrix(stiff_ref, stiff_w)
            tmp[...] = jnp.zeros_like(tmp)
            for h in range(3):
                split_store(h * FROWS, rot_ref[h], FROWS)
            rot_w[...] = tmp[0:80, 0:80].astype(BF16)
            tmp[...] = jnp.zeros_like(tmp)
            for h in range(3):
                back = jnp.transpose(rot_ref[h])
                for i in range(FACE):
                    at = (i // 3) * 8 + 5 + i % 3
                    tmp[at : at + 1, h * FROWS : h * FROWS + FACE] = back[i : i + 1, :]
            last = jnp.transpose(tmp[0:BASIS, 0:ELEMS])[0:80]
            tmp[...] = jnp.zeros_like(tmp)
            split_store(0, last, BASIS)
            rot_last_w[...] = tmp[0:80, 0:176].astype(BF16)
            tmp[...] = jnp.zeros_like(tmp)
            face_matrix(lift_ref)
            high = tmp[0:96, 0:BASIS]
            lift_w[...] = jnp.transpose(
                jnp.concatenate([high, low_of(high), high], axis=0)
            ).astype(BF16)
            face_rows = lax.broadcasted_iota(jnp.int32, (FACES, ELEMS), 0)
            for f in range(4):
                near = near_ref[f : f + 1, :]
                source = jnp.where(near >= 0, near_face_ref[f : f + 1, :] * ELEMS + near, -1)
                near_w[:, f * ELEMS : (f + 1) * ELEMS] = (
                    (face_rows == source).astype(F32).astype(BF16)
                )
            outside = jnp.concatenate([near_ref[f : f + 1, :] < 0 for f in range(4)], axis=1)
            take_ids = jnp.transpose(recv_list_ref[0, 0])
            one_hot([take_ids], take_w, outside)
            one_hot(halves(take_ids), take_half_w, outside)
        orient = jnp.concatenate([ori_ref[f : f + 1, :] for f in range(4)], axis=1)
        slopes = dot(stiff_w[...], whole)
        volume = stress_from(slopes[:, 6 * ELEMS :], -1.0) + speed_from(slopes[:, : 6 * ELEMS], -1.0)
        for q in range(QUANT):
            out_ref[q] = current[q] + volume[q]
        beside = dot(faces_high, near_w[...]) + dot(faces_low, near_w[...])

        for part in range(2):
            for d in FAR_FIRST[::-1]:
                pl.when(exists[7 - d])(copies[part, d].wait_recv)
        first = jnp.transpose(jnp.concatenate([recv_first[step, d] for d in range(8)], axis=0))
        rest = jnp.transpose(jnp.concatenate([recv_rest[step, d] for d in range(8)], axis=0))
        rest = jnp.concatenate([rest[0:REST], rest[REST:]], axis=1)
        arrived_faces = []
        for got, take in ((first, take_w), (rest, take_half_w)):
            got_high = got.astype(BF16)
            got_low = (got - got_high.astype(F32)).astype(BF16)
            arrived_faces.append(dot(got_high, take[...]) + dot(got_low, take[...]))
        beside = beside + jnp.concatenate(arrived_faces, axis=0)

        turned = []
        for q in range(QUANT):
            if q < QUANT - 1:
                block = beside[q * FROWS : (q + 1) * FROWS]
                matrix = rot_w
            else:
                block = jnp.concatenate(
                    [beside[b * FROWS + 16 : (b + 1) * FROWS] for b in range(7)], axis=0
                )
                matrix = rot_last_w
            right = jnp.concatenate(
                [block, block, low_of(block), jnp.zeros((8, FACES), F32)], axis=0
            )
            each = dot(matrix[...], right.astype(BF16))
            turned.append(
                jnp.where(
                    orient == 0,
                    each[0:FROWS],
                    jnp.where(orient == 1, each[FROWS : 2 * FROWS], each[2 * FROWS : 3 * FROWS]),
                )
            )

        fluxes = [[] for _ in range(QUANT)]
        for f in range(4):
            here = slice(f * ELEMS, (f + 1) * ELEMS)
            n = [nrm_ref[k, f : f + 1, :] for k in range(3)]
            both = []
            apart = []
            for q in range(QUANT):
                mine = own[f * FROWS : (f + 1) * FROWS, q * ELEMS : (q + 1) * ELEMS]
                theirs = turned[q][:, here]
                both.append(mine + theirs)
                apart.append(mine - theirs)
            half = 0.5 * root * (jnp.abs(n[0]) + jnp.abs(n[1]) + jnp.abs(n[2]))
            u, v, w = both[6:]
            ns = [-0.5 * shear * x for x in n]
            spread = (-0.5 * lame) * (n[0] * u + n[1] * v + n[2] * w)
            over = [-0.5 * inverse * x for x in n]
            xx, yy, zz, xy, yz, xz = both[:6]
            flux = [
                spread + (2.0 * ns[0]) * u,
                spread + (2.0 * ns[1]) * v,
                spread + (2.0 * ns[2]) * w,
                ns[0] * v + ns[1] * u,
                ns[1] * w + ns[2] * v,
                ns[0] * w + ns[2] * u,
                over[0] * xx + over[1] * xy + over[2] * xz,
                over[0] * xy + over[1] * yy + over[2] * yz,
                over[0] * xz + over[1] * yz + over[2] * zz,
            ]
            for q in range(QUANT):
                fluxes[q].append(flux[q] + half * apart[q])
        lifted = dot(
            lift_w[...], stacked([jnp.concatenate(parts, axis=0) for parts in fluxes], 96)
        )
        for q in range(QUANT):
            out_ref[q] = out_ref[q] - lifted[:, q * ELEMS : (q + 1) * ELEMS]
        for part in range(2):
            for d in range(8):
                pl.when(exists[d])(copies[part, d].wait_send)


def solution(mesh):
    rows, cols = mesh.shape["prow"], mesh.shape["pcol"]

    def per_device(*args):
        args = list(args)
        args[3] = args[3].transpose(1, 0, 2)
        args[4] = args[4].transpose(2, 0, 1)
        args[6] = args[6].transpose(1, 0)
        args[7] = args[7].reshape(1, ELEMS)
        args[9] = args[9].transpose(1, 0, 2)
        vmem = pl.BlockSpec(memory_space=pltpu.VMEM)
        return pl.pallas_call(
            functools.partial(kernel, rows, cols),
            out_shape=pltpu.VMEM((QUANT, BASIS, ELEMS), F32),
            in_specs=[pl.BlockSpec(memory_space=pltpu.HBM)] * 15,
            out_specs=vmem,
            scratch_shapes=[pltpu.VMEM(x.shape, x.dtype) for x in args]
            + [
                pltpu.SemaphoreType.DMA((15,)),
                pltpu.VMEM((224, 384), F32),
                pltpu.VMEM((176, 3 * KBLOCK), BF16),
                pltpu.VMEM((176, 3 * KBLOCK), BF16),
                pltpu.VMEM((96, 3 * KBLOCK), BF16),
                pltpu.VMEM((224, 3 * KBLOCK), BF16),
                pltpu.VMEM((BASIS, 288), BF16),
                pltpu.VMEM((80, 80), BF16),
                pltpu.VMEM((80, 176), BF16),
                pltpu.VMEM((FACES, FACES), BF16),
                pltpu.VMEM((8 * SLOTS, FACES), BF16),
                pltpu.VMEM((2 * 8 * HROWS, FACES), BF16),
                pltpu.VMEM((8 * SLOTS, FACES), BF16),
                pltpu.VMEM((2 * 8 * HROWS, FACES), BF16),
                pltpu.VMEM((STEPS, 8, SLOTS, ELEMS), F32),
                pltpu.VMEM((STEPS, 8, HROWS, ELEMS), F32),
                pltpu.VMEM((STEPS, 8, SLOTS, ELEMS), F32),
                pltpu.VMEM((STEPS, 8, HROWS, ELEMS), F32),
                pltpu.SemaphoreType.DMA((STEPS, 2, 8)),
                pltpu.SemaphoreType.DMA((STEPS, 2, 8)),
            ],
            compiler_params=pltpu.CompilerParams(
                collective_id=0, has_side_effects=True, vmem_limit_bytes=40 * 1024 * 1024
            ),
        )(*[pltpu.with_memory_space_constraint(x, pltpu.HBM) for x in args])

    both = ("prow", "pcol")
    return jax.shard_map(
        per_device,
        mesh=mesh,
        in_specs=(
            P(None, None, both),
            P(),
            P(),
            P(),
            P(),
            P(),
            P(),
            P(both),
            P(None, None, both),
            P(None, None, both),
            P(None, both),
            P(None, both),
            P(None, both),
            P("prow", "pcol", None, None),
            P("prow", "pcol", None, None),
        ),
        out_specs=P(None, None, both),
        check_vma=False,
    )
```

```python
import functools

import jax
import jax.numpy as jnp
from jax import lax
from jax.experimental import pallas as pl
from jax.experimental.pallas import tpu as pltpu
from jax.sharding import PartitionSpec as P

ORDER = 6
STEPS = 2
TIME_STEP = 0.8
OFFSETS = ((-1, -1), (-1, 0), (-1, 1), (0, -1), (0, 1), (1, -1), (1, 0), (1, 1))
FAR_FIRST = (0, 2, 5, 7, 3, 4, 1, 6)
MESH = pl.DeviceIdType.MESH
F32 = jnp.float32
BF16 = jnp.bfloat16
QUANT = 9
BASIS = 56
KBLOCK = 64
FACE = 21
FROWS = 24
ELEMS = 128
FACES = 4 * ELEMS
SLOTS = 24
WIDE = 256


(
    GRAD,
    DOF,
    JAC,
    MAT,
    MID,
    PROJ,
    SEND_LIST,
    STIFF,
    LIFT,
    ROT,
    NRM,
    ORI,
    NEAR,
    NEAR_FACE,
    RECV_LIST,
) = range(15)


def dot(a, b):
    return lax.dot_general(a, b, (((1,), (0,)), ((), ())), preferred_element_type=F32)


def dot_nt(a, b):
    return lax.dot_general(a, b, (((1,), (1,)), ((), ())), preferred_element_type=F32)


def low_of(x):
    return x - x.astype(BF16).astype(F32)


def widen(x, rows):
    if x.shape[0] == rows:
        return x
    return jnp.concatenate([x, jnp.zeros((rows - x.shape[0], x.shape[1]), F32)], axis=0)


def stacked(slabs, rows):
    columns = []
    for slab in slabs:
        full = widen(slab, rows)
        high = full.astype(BF16)
        low = (full - high.astype(F32)).astype(BF16)
        columns.append(jnp.concatenate([high, high, low], axis=0))
    return jnp.concatenate(columns, axis=1)


def stress_rates(ux, vy, wz, uv, vw, uw, lame, shear2, shear):
    spread = lame * (ux + vy + wz)
    return [
        spread + shear2 * ux,
        spread + shear2 * vy,
        spread + shear2 * wz,
        shear * uv,
        shear * vw,
        shear * uw,
    ]


def kernel(
    rows,
    cols,
    dof_hbm,
    grad_hbm,
    stiff_hbm,
    proj_hbm,
    lift_hbm,
    rot_hbm,
    mat_hbm,
    mid_hbm,
    jac_hbm,
    nrm_hbm,
    ori_hbm,
    near_hbm,
    near_face_hbm,
    send_list_hbm,
    recv_list_hbm,
    out_ref,
    dof_ref,
    grad_ref,
    stiff_ref,
    proj_ref,
    lift_ref,
    rot_ref,
    mat_ref,
    mid_ref,
    jac_ref,
    nrm_ref,
    ori_ref,
    near_ref,
    near_face_ref,
    send_list_ref,
    recv_list_ref,
    load_sem,
    tmp,
    grad_w,
    stiff_w,
    proj_w,
    lift_w,
    rot_w,
    near_w,
    give_w,
    take_w,
    send_buf,
    recv_buf,
    send_sem,
    recv_sem,
):
    loads = []
    for at, (source, dest) in enumerate(
        [
            (grad_hbm, grad_ref),
            (dof_hbm, dof_ref),
            (jac_hbm, jac_ref),
            (mat_hbm, mat_ref),
            (mid_hbm, mid_ref),
            (proj_hbm, proj_ref),
            (send_list_hbm, send_list_ref),
            (stiff_hbm, stiff_ref),
            (lift_hbm, lift_ref),
            (rot_hbm, rot_ref),
            (nrm_hbm, nrm_ref),
            (ori_hbm, ori_ref),
            (near_hbm, near_ref),
            (near_face_hbm, near_face_ref),
            (recv_list_hbm, recv_list_ref),
        ]
    ):
        load = pltpu.make_async_copy(source, dest, load_sem.at[at])
        load.start()
        loads.append(load)

    row = lax.axis_index("prow")
    col = lax.axis_index("pcol")
    partners = []
    exists = []
    for dr, dc in OFFSETS:
        there = [row + dr, col + dc]
        inside = []
        if dr:
            inside.append(there[0] >= 0 if dr < 0 else there[0] < rows)
        if dc:
            inside.append(there[1] >= 0 if dc < 0 else there[1] < cols)
        partners.append((there[0], there[1]))
        exists.append(functools.reduce(jnp.logical_and, inside))
    up_down = (row > 0).astype(jnp.int32) + (row < rows - 1).astype(jnp.int32)
    left_right = (col > 0).astype(jnp.int32) + (col < cols - 1).astype(jnp.int32)
    peers = up_down + left_right + up_down * left_right
    barrier = pltpu.get_barrier_semaphore()
    for d in range(8):

        @pl.when(exists[d])
        def _(d=d):
            pl.semaphore_signal(barrier, inc=1, device_id=partners[d], device_id_type=MESH)

        @pl.when(jnp.logical_not(exists[d]))
        def _(d=d):
            for step in range(STEPS):
                recv_buf[step, d] = jnp.zeros((SLOTS, WIDE), F32)

    def arrived(*names):
        for name in names:
            loads[name].wait()

    def split_store(at, block, step_k):
        height, width = block.shape
        low = low_of(block)
        tmp[at : at + height, 0:width] = block
        tmp[at : at + height, step_k : step_k + width] = low
        tmp[at : at + height, 2 * step_k : 2 * step_k + width] = block

    def derivative_matrix(source, dest):
        for block in range(7):
            for d in range(3):
                split_store(block * 24 + d * 8, source[d, block * 8 : block * 8 + 8], KBLOCK)
        dest[...] = tmp[0:176, 0 : 3 * KBLOCK].astype(BF16)

    def face_matrix(source):
        for f in range(4):
            for i in range(FACE):
                tmp[f * FROWS + i : f * FROWS + i + 1, 0:BASIS] = source[i, f : f + 1, :]

    def one_hot(ids_ref, dest, keep):
        ids = jnp.transpose(ids_ref[0, 0])
        face_ids = lax.broadcasted_iota(jnp.int32, (SLOTS, FACES), 1)
        parts = []
        for d in range(8):
            hit = ids[:, d : d + 1] == face_ids
            if keep is not None:
                hit = hit & keep
            parts.append(jnp.where(hit, 1.0, 0.0).astype(F32))
        dest[...] = jnp.concatenate(parts, axis=0).astype(BF16)

    tmp[...] = jnp.zeros_like(tmp)
    arrived(GRAD)
    derivative_matrix(grad_ref, grad_w)

    arrived(JAC, MAT, MID)
    hot = lax.broadcasted_iota(jnp.int32, (16, ELEMS), 0) == mid_ref[...]
    table = jnp.transpose(mat_ref[...])
    density, lame, shear = [
        jnp.sum(jnp.where(hot, table[:, j : j + 1], 0.0), axis=0, keepdims=True) for j in range(3)
    ]
    inverse = 1.0 / density
    lame8, shear8, inverse8 = [
        jnp.broadcast_to(x, (8, ELEMS)) for x in (lame, shear, inverse)
    ]
    jac = [
        [jnp.broadcast_to(jac_ref[d, k : k + 1, :], (8, ELEMS)) for k in range(3)]
        for d in range(3)
    ]
    arrived(DOF, PROJ, SEND_LIST)
    root = jnp.sqrt((lame + 2.0 * shear) * inverse)

    def along(slopes, block):
        def one(place, k):
            parts = [
                jac[d][k]
                * slopes[
                    block * 24 + d * 8 : block * 24 + d * 8 + 8,
                    place * ELEMS : (place + 1) * ELEMS,
                ]
                for d in range(3)
            ]
            return parts[0] + parts[1] + parts[2]

        return one

    def by_blocks(rates):
        return [jnp.concatenate(list(x), axis=0) for x in zip(*[rates(b) for b in range(7)])]

    def stress_from(slopes, scale):
        lame_s, shear2_s, shear_s = scale * lame8, (2.0 * scale) * shear8, scale * shear8

        def rates(block):
            one = along(slopes, block)
            ux, vy, wz = one(0, 0), one(1, 1), one(2, 2)
            uv = one(1, 0) + one(0, 1)
            vw = one(2, 1) + one(1, 2)
            uw = one(2, 0) + one(0, 2)
            return stress_rates(ux, vy, wz, uv, vw, uw, lame_s, shear2_s, shear_s)

        return by_blocks(rates)

    def speed_from(slopes, scale):
        over = scale * inverse8

        def rates(block):
            one = along(slopes, block)
            return [
                over * (one(0, 0) + one(3, 1) + one(5, 2)),
                over * (one(3, 0) + one(1, 1) + one(4, 2)),
                over * (one(5, 0) + one(4, 1) + one(2, 2)),
            ]

        return by_blocks(rates)

    for step in range(STEPS):
        current = dof_ref if step == 0 else out_ref
        level = [TIME_STEP * current[q] for q in range(QUANT)]
        total = list(level)
        of_speed = dot(grad_w[...], stacked(level[6:], KBLOCK))
        of_stress = dot(grad_w[...], stacked(level[:6], KBLOCK))
        for power in range(1, ORDER):
            scale = TIME_STEP / (power + 1)
            stress = stress_from(of_speed, scale)
            if power < ORDER - 1:
                next_of_stress = dot(grad_w[...], stacked(stress, KBLOCK))
            speed = speed_from(of_stress, scale)
            if power < ORDER - 1:
                of_speed = dot(grad_w[...], stacked(speed, KBLOCK))
                of_stress = next_of_stress
            total = [t + x for t, x in zip(total, stress + speed)]

        if step == 0:
            tmp[...] = jnp.zeros_like(tmp)
            face_matrix(proj_ref)
            split_store(0, tmp[0:96, 0:KBLOCK], KBLOCK)
            proj_w[...] = tmp[0:96, 0 : 3 * KBLOCK].astype(BF16)
            one_hot(send_list_ref, give_w, None)
        whole = stacked(total, KBLOCK)
        own = dot(proj_w[...], whole)
        faces = jnp.concatenate(
            [
                jnp.concatenate(
                    [
                        own[f * FROWS : (f + 1) * FROWS, q * ELEMS : (q + 1) * ELEMS]
                        for f in range(4)
                    ],
                    axis=1,
                )
                for q in range(QUANT)
            ]
            + [jnp.zeros((WIDE - QUANT * FROWS, FACES), F32)],
            axis=0,
        )
        faces_high = faces.astype(BF16)
        faces_low = (faces - faces_high.astype(F32)).astype(BF16)
        outgoing = dot_nt(give_w[...], faces_high) + dot_nt(give_w[...], faces_low)
        for d in range(8):
            send_buf[step, d] = outgoing[d * SLOTS : (d + 1) * SLOTS]
        if step == 0:
            pl.semaphore_wait(barrier, peers)
        copies = [None] * 8
        for d in FAR_FIRST:
            copy = pltpu.make_async_remote_copy(
                src_ref=send_buf.at[step, d],
                dst_ref=recv_buf.at[step, 7 - d],
                send_sem=send_sem.at[step, d],
                recv_sem=recv_sem.at[step, 7 - d],
                device_id=partners[d],
                device_id_type=MESH,
            )
            copies[d] = copy
            pl.when(exists[d])(copy.start)

        if step == 0:
            arrived(STIFF, LIFT, ROT, NRM, ORI, NEAR, NEAR_FACE, RECV_LIST)
            derivative_matrix(stiff_ref, stiff_w)
            tmp[...] = jnp.zeros_like(tmp)
            for h in range(3):
                split_store(h * FROWS, rot_ref[h], FROWS)
            rot_w[...] = tmp[0:80, 0:80].astype(BF16)
            tmp[...] = jnp.zeros_like(tmp)
            face_matrix(lift_ref)
            high = tmp[0:96, 0:BASIS]
            lift_w[...] = jnp.transpose(
                jnp.concatenate([high, low_of(high), high], axis=0)
            ).astype(BF16)
            face_rows = lax.broadcasted_iota(jnp.int32, (FACES, ELEMS), 0)
            for f in range(4):
                near = near_ref[f : f + 1, :]
                source = jnp.where(near >= 0, near_face_ref[f : f + 1, :] * ELEMS + near, -1)
                near_w[:, f * ELEMS : (f + 1) * ELEMS] = (
                    (face_rows == source).astype(F32).astype(BF16)
                )
            outside = jnp.concatenate([near_ref[f : f + 1, :] < 0 for f in range(4)], axis=1)
            one_hot(recv_list_ref, take_w, outside)
        orient = jnp.concatenate([ori_ref[f : f + 1, :] for f in range(4)], axis=1)
        slopes = dot(stiff_w[...], whole)
        volume = stress_from(slopes[:, 6 * ELEMS :], -1.0) + speed_from(slopes[:, : 6 * ELEMS], -1.0)
        for q in range(QUANT):
            out_ref[q] = current[q] + volume[q]
        beside = dot(faces_high, near_w[...]) + dot(faces_low, near_w[...])

        for d in range(8):
            pl.when(exists[d])(copies[d].wait_send)
        for d in FAR_FIRST[::-1]:
            pl.when(exists[7 - d])(copies[d].wait_recv)
        got = jnp.transpose(
            jnp.concatenate([recv_buf[step, d] for d in range(8)], axis=0)
        )
        got_high = got.astype(BF16)
        got_low = (got - got_high.astype(F32)).astype(BF16)
        beside = beside + dot(got_high, take_w[...]) + dot(got_low, take_w[...])

        turned = []
        for q in range(QUANT):
            block = beside[q * FROWS : (q + 1) * FROWS]
            low = low_of(block)
            right = jnp.concatenate([block, block, low, jnp.zeros((8, FACES), F32)], axis=0)
            each = dot(rot_w[...], right.astype(BF16))
            turned.append(
                jnp.where(
                    orient == 0,
                    each[0:FROWS],
                    jnp.where(orient == 1, each[FROWS : 2 * FROWS], each[2 * FROWS : 3 * FROWS]),
                )
            )

        fluxes = [[] for _ in range(QUANT)]
        for f in range(4):
            here = slice(f * ELEMS, (f + 1) * ELEMS)
            n = [nrm_ref[k, f : f + 1, :] for k in range(3)]
            both = []
            apart = []
            for q in range(QUANT):
                mine = own[f * FROWS : (f + 1) * FROWS, q * ELEMS : (q + 1) * ELEMS]
                theirs = turned[q][:, here]
                both.append(mine + theirs)
                apart.append(mine - theirs)
            half = 0.5 * root * (jnp.abs(n[0]) + jnp.abs(n[1]) + jnp.abs(n[2]))
            u, v, w = both[6:]
            ns = [-0.5 * shear * x for x in n]
            spread = (-0.5 * lame) * (n[0] * u + n[1] * v + n[2] * w)
            over = [-0.5 * inverse * x for x in n]
            xx, yy, zz, xy, yz, xz = both[:6]
            flux = [
                spread + (2.0 * ns[0]) * u,
                spread + (2.0 * ns[1]) * v,
                spread + (2.0 * ns[2]) * w,
                ns[0] * v + ns[1] * u,
                ns[1] * w + ns[2] * v,
                ns[0] * w + ns[2] * u,
                over[0] * xx + over[1] * xy + over[2] * xz,
                over[0] * xy + over[1] * yy + over[2] * yz,
                over[0] * xz + over[1] * yz + over[2] * zz,
            ]
            for q in range(QUANT):
                fluxes[q].append(flux[q] + half * apart[q])
        lifted = dot(
            lift_w[...], stacked([jnp.concatenate(parts, axis=0) for parts in fluxes], 96)
        )
        for q in range(QUANT):
            out_ref[q] = out_ref[q] - lifted[:, q * ELEMS : (q + 1) * ELEMS]


def solution(mesh):
    rows, cols = mesh.shape["prow"], mesh.shape["pcol"]

    def per_device(*args):
        args = list(args)
        args[3] = args[3].transpose(1, 0, 2)
        args[4] = args[4].transpose(2, 0, 1)
        args[6] = args[6].transpose(1, 0)
        args[7] = args[7].reshape(1, ELEMS)
        args[9] = args[9].transpose(1, 0, 2)
        vmem = pl.BlockSpec(memory_space=pltpu.VMEM)
        return pl.pallas_call(
            functools.partial(kernel, rows, cols),
            out_shape=pltpu.VMEM((QUANT, BASIS, ELEMS), F32),
            in_specs=[pl.BlockSpec(memory_space=pltpu.HBM)] * 15,
            out_specs=vmem,
            scratch_shapes=[pltpu.VMEM(x.shape, x.dtype) for x in args]
            + [
                pltpu.SemaphoreType.DMA((15,)),
                pltpu.VMEM((176, 384), F32),
                pltpu.VMEM((176, 3 * KBLOCK), BF16),
                pltpu.VMEM((176, 3 * KBLOCK), BF16),
                pltpu.VMEM((96, 3 * KBLOCK), BF16),
                pltpu.VMEM((BASIS, 288), BF16),
                pltpu.VMEM((80, 80), BF16),
                pltpu.VMEM((FACES, FACES), BF16),
                pltpu.VMEM((8 * SLOTS, FACES), BF16),
                pltpu.VMEM((8 * SLOTS, FACES), BF16),
                pltpu.VMEM((STEPS, 8, SLOTS, WIDE), F32),
                pltpu.VMEM((STEPS, 8, SLOTS, WIDE), F32),
                pltpu.SemaphoreType.DMA((STEPS, 8)),
                pltpu.SemaphoreType.DMA((STEPS, 8)),
            ],
            compiler_params=pltpu.CompilerParams(
                collective_id=0, has_side_effects=True, vmem_limit_bytes=40 * 1024 * 1024
            ),
        )(*[pltpu.with_memory_space_constraint(x, pltpu.HBM) for x in args])

    both = ("prow", "pcol")
    return jax.shard_map(
        per_device,
        mesh=mesh,
        in_specs=(
            P(None, None, both),
            P(),
            P(),
            P(),
            P(),
            P(),
            P(),
            P(both),
            P(None, None, both),
            P(None, None, both),
            P(None, both),
            P(None, both),
            P(None, both),
            P("prow", "pcol", None, None),
            P("prow", "pcol", None, None),
        ),
        out_specs=P(None, None, both),
        check_vma=False,
    )
```

```python
import functools

import jax
import jax.numpy as jnp
from jax import lax
from jax.experimental import pallas as pl
from jax.experimental.pallas import tpu as pltpu
from jax.sharding import PartitionSpec as P

ORDER = 6
STEPS = 2
TIME_STEP = 0.8
OFFSETS = ((-1, -1), (-1, 0), (-1, 1), (0, -1), (0, 1), (1, -1), (1, 0), (1, 1))
FAR_FIRST = (0, 2, 5, 7, 3, 4, 1, 6)
MESH = pl.DeviceIdType.MESH
F32 = jnp.float32
BF16 = jnp.bfloat16
QUANT = 9
BASIS = 56
KBLOCK = 64
FACE = 21
FROWS = 24
ELEMS = 128
FACES = 4 * ELEMS
SLOTS = 24
WIDE = 256


(
    GRAD,
    DOF,
    JAC,
    MAT,
    MID,
    PROJ,
    SEND_LIST,
    STIFF,
    LIFT,
    ROT,
    NRM,
    ORI,
    NEAR,
    NEAR_FACE,
    RECV_LIST,
) = range(15)


def dot(a, b):
    return lax.dot_general(a, b, (((1,), (0,)), ((), ())), preferred_element_type=F32)


def dot_nt(a, b):
    return lax.dot_general(a, b, (((1,), (1,)), ((), ())), preferred_element_type=F32)


def low_of(x):
    return x - x.astype(BF16).astype(F32)


def widen(x, rows):
    if x.shape[0] == rows:
        return x
    return jnp.concatenate([x, jnp.zeros((rows - x.shape[0], x.shape[1]), F32)], axis=0)


def stacked(slabs, rows):
    columns = []
    for slab in slabs:
        full = widen(slab, rows)
        high = full.astype(BF16)
        low = (full - high.astype(F32)).astype(BF16)
        columns.append(jnp.concatenate([high, high, low], axis=0))
    return jnp.concatenate(columns, axis=1)


def stress_rates(ux, vy, wz, uv, vw, uw, lame, shear2, shear):
    spread = lame * (ux + vy + wz)
    return [
        spread + shear2 * ux,
        spread + shear2 * vy,
        spread + shear2 * wz,
        shear * uv,
        shear * vw,
        shear * uw,
    ]


def kernel(
    rows,
    cols,
    dof_hbm,
    grad_hbm,
    stiff_hbm,
    proj_hbm,
    lift_hbm,
    rot_hbm,
    mat_hbm,
    mid_hbm,
    jac_hbm,
    nrm_hbm,
    ori_hbm,
    near_hbm,
    near_face_hbm,
    send_list_hbm,
    recv_list_hbm,
    out_ref,
    dof_ref,
    grad_ref,
    stiff_ref,
    proj_ref,
    lift_ref,
    rot_ref,
    mat_ref,
    mid_ref,
    jac_ref,
    nrm_ref,
    ori_ref,
    near_ref,
    near_face_ref,
    send_list_ref,
    recv_list_ref,
    load_sem,
    tmp,
    grad_w,
    stiff_w,
    proj_w,
    lift_w,
    rot_w,
    near_w,
    give_w,
    take_w,
    send_buf,
    recv_buf,
    send_sem,
    recv_sem,
):
    loads = []
    for at, (source, dest) in enumerate(
        [
            (grad_hbm, grad_ref),
            (dof_hbm, dof_ref),
            (jac_hbm, jac_ref),
            (mat_hbm, mat_ref),
            (mid_hbm, mid_ref),
            (proj_hbm, proj_ref),
            (send_list_hbm, send_list_ref),
            (stiff_hbm, stiff_ref),
            (lift_hbm, lift_ref),
            (rot_hbm, rot_ref),
            (nrm_hbm, nrm_ref),
            (ori_hbm, ori_ref),
            (near_hbm, near_ref),
            (near_face_hbm, near_face_ref),
            (recv_list_hbm, recv_list_ref),
        ]
    ):
        load = pltpu.make_async_copy(source, dest, load_sem.at[at])
        loads.append(load)
    for load in loads[:2]:
        load.start()

    row = lax.axis_index("prow")
    col = lax.axis_index("pcol")
    partners = []
    exists = []
    for dr, dc in OFFSETS:
        there = [row + dr, col + dc]
        inside = []
        if dr:
            inside.append(there[0] >= 0 if dr < 0 else there[0] < rows)
        if dc:
            inside.append(there[1] >= 0 if dc < 0 else there[1] < cols)
        partners.append((there[0], there[1]))
        exists.append(functools.reduce(jnp.logical_and, inside))
    up_down = (row > 0).astype(jnp.int32) + (row < rows - 1).astype(jnp.int32)
    left_right = (col > 0).astype(jnp.int32) + (col < cols - 1).astype(jnp.int32)
    peers = up_down + left_right + up_down * left_right
    barrier = pltpu.get_barrier_semaphore()
    for d in range(8):

        @pl.when(exists[d])
        def _(d=d):
            pl.semaphore_signal(barrier, inc=1, device_id=partners[d], device_id_type=MESH)

        @pl.when(jnp.logical_not(exists[d]))
        def _(d=d):
            for step in range(STEPS):
                recv_buf[step, d] = jnp.zeros((SLOTS, WIDE), F32)

    for load in loads[2:]:
        load.start()

    def arrived(*names):
        for name in names:
            loads[name].wait()

    def split_store(at, block, step_k):
        height, width = block.shape
        low = low_of(block)
        tmp[at : at + height, 0:width] = block
        tmp[at : at + height, step_k : step_k + width] = low
        tmp[at : at + height, 2 * step_k : 2 * step_k + width] = block

    def derivative_matrix(source, dest):
        for block in range(7):
            for d in range(3):
                split_store(block * 24 + d * 8, source[d, block * 8 : block * 8 + 8], KBLOCK)
        dest[...] = tmp[0:176, 0 : 3 * KBLOCK].astype(BF16)

    def face_matrix(source):
        for f in range(4):
            for i in range(FACE):
                tmp[f * FROWS + i : f * FROWS + i + 1, 0:BASIS] = source[i, f : f + 1, :]

    def one_hot(ids_ref, dest, keep):
        ids = jnp.transpose(ids_ref[0, 0])
        face_ids = lax.broadcasted_iota(jnp.int32, (SLOTS, FACES), 1)
        parts = []
        for d in range(8):
            hit = ids[:, d : d + 1] == face_ids
            if keep is not None:
                hit = hit & keep
            parts.append(jnp.where(hit, 1.0, 0.0).astype(F32))
        dest[...] = jnp.concatenate(parts, axis=0).astype(BF16)

    tmp[...] = jnp.zeros_like(tmp)
    arrived(GRAD)
    derivative_matrix(grad_ref, grad_w)

    arrived(JAC, MAT, MID)
    hot = lax.broadcasted_iota(jnp.int32, (16, ELEMS), 0) == mid_ref[...]
    table = jnp.transpose(mat_ref[...])
    density, lame, shear = [
        jnp.sum(jnp.where(hot, table[:, j : j + 1], 0.0), axis=0, keepdims=True) for j in range(3)
    ]
    inverse = 1.0 / density
    lame8, shear8, inverse8 = [
        jnp.broadcast_to(x, (8, ELEMS)) for x in (lame, shear, inverse)
    ]
    jac = [
        [jnp.broadcast_to(jac_ref[d, k : k + 1, :], (8, ELEMS)) for k in range(3)]
        for d in range(3)
    ]
    arrived(DOF, PROJ, SEND_LIST)
    root = jnp.sqrt((lame + 2.0 * shear) * inverse)

    def along(slopes, block):
        def one(place, k):
            parts = [
                jac[d][k]
                * slopes[
                    block * 24 + d * 8 : block * 24 + d * 8 + 8,
                    place * ELEMS : (place + 1) * ELEMS,
                ]
                for d in range(3)
            ]
            return parts[0] + parts[1] + parts[2]

        return one

    def by_blocks(rates):
        return [jnp.concatenate(list(x), axis=0) for x in zip(*[rates(b) for b in range(7)])]

    def stress_from(slopes, scale):
        lame_s, shear2_s, shear_s = scale * lame8, (2.0 * scale) * shear8, scale * shear8

        def rates(block):
            one = along(slopes, block)
            ux, vy, wz = one(0, 0), one(1, 1), one(2, 2)
            uv = one(1, 0) + one(0, 1)
            vw = one(2, 1) + one(1, 2)
            uw = one(2, 0) + one(0, 2)
            return stress_rates(ux, vy, wz, uv, vw, uw, lame_s, shear2_s, shear_s)

        return by_blocks(rates)

    def speed_from(slopes, scale):
        over = scale * inverse8

        def rates(block):
            one = along(slopes, block)
            return [
                over * (one(0, 0) + one(3, 1) + one(5, 2)),
                over * (one(3, 0) + one(1, 1) + one(4, 2)),
                over * (one(5, 0) + one(4, 1) + one(2, 2)),
            ]

        return by_blocks(rates)

    for step in range(STEPS):
        current = dof_ref if step == 0 else out_ref
        level = [TIME_STEP * current[q] for q in range(QUANT)]
        total = list(level)
        of_speed = dot(grad_w[...], stacked(level[6:], KBLOCK))
        of_stress = dot(grad_w[...], stacked(level[:6], KBLOCK))
        for power in range(1, ORDER):
            scale = TIME_STEP / (power + 1)
            stress = stress_from(of_speed, scale)
            if power < ORDER - 1:
                next_of_stress = dot(grad_w[...], stacked(stress, KBLOCK))
            speed = speed_from(of_stress, scale)
            if power < ORDER - 1:
                of_speed = dot(grad_w[...], stacked(speed, KBLOCK))
                of_stress = next_of_stress
            total = [t + x for t, x in zip(total, stress + speed)]

        if step == 0:
            tmp[...] = jnp.zeros_like(tmp)
            face_matrix(proj_ref)
            split_store(0, tmp[0:96, 0:KBLOCK], KBLOCK)
            proj_w[...] = tmp[0:96, 0 : 3 * KBLOCK].astype(BF16)
            one_hot(send_list_ref, give_w, None)
        whole = stacked(total, KBLOCK)
        own = dot(proj_w[...], whole)
        faces = jnp.concatenate(
            [
                jnp.concatenate(
                    [
                        own[f * FROWS : (f + 1) * FROWS, q * ELEMS : (q + 1) * ELEMS]
                        for f in range(4)
                    ],
                    axis=1,
                )
                for q in range(QUANT)
            ]
            + [jnp.zeros((WIDE - QUANT * FROWS, FACES), F32)],
            axis=0,
        )
        faces_high = faces.astype(BF16)
        faces_low = (faces - faces_high.astype(F32)).astype(BF16)
        outgoing = dot_nt(give_w[...], faces_high) + dot_nt(give_w[...], faces_low)
        for d in range(8):
            send_buf[step, d] = outgoing[d * SLOTS : (d + 1) * SLOTS]
        if step == 0:
            pl.semaphore_wait(barrier, peers)
        copies = [None] * 8
        for d in FAR_FIRST:
            copy = pltpu.make_async_remote_copy(
                src_ref=send_buf.at[step, d],
                dst_ref=recv_buf.at[step, 7 - d],
                send_sem=send_sem.at[step, d],
                recv_sem=recv_sem.at[step, 7 - d],
                device_id=partners[d],
                device_id_type=MESH,
            )
            copies[d] = copy
            pl.when(exists[d])(copy.start)

        if step == 0:
            arrived(STIFF, LIFT, ROT, NRM, ORI, NEAR, NEAR_FACE, RECV_LIST)
            derivative_matrix(stiff_ref, stiff_w)
            tmp[...] = jnp.zeros_like(tmp)
            for h in range(3):
                split_store(h * FROWS, rot_ref[h], FROWS)
            rot_w[...] = tmp[0:80, 0:80].astype(BF16)
            tmp[...] = jnp.zeros_like(tmp)
            face_matrix(lift_ref)
            high = tmp[0:96, 0:BASIS]
            lift_w[...] = jnp.transpose(
                jnp.concatenate([high, low_of(high), high], axis=0)
            ).astype(BF16)
            face_rows = lax.broadcasted_iota(jnp.int32, (FACES, ELEMS), 0)
            for f in range(4):
                near = near_ref[f : f + 1, :]
                source = jnp.where(near >= 0, near_face_ref[f : f + 1, :] * ELEMS + near, -1)
                near_w[:, f * ELEMS : (f + 1) * ELEMS] = (
                    (face_rows == source).astype(F32).astype(BF16)
                )
            outside = jnp.concatenate([near_ref[f : f + 1, :] < 0 for f in range(4)], axis=1)
            one_hot(recv_list_ref, take_w, outside)
        orient = jnp.concatenate([ori_ref[f : f + 1, :] for f in range(4)], axis=1)
        slopes = dot(stiff_w[...], whole)
        volume = stress_from(slopes[:, 6 * ELEMS :], -1.0) + speed_from(slopes[:, : 6 * ELEMS], -1.0)
        for q in range(QUANT):
            out_ref[q] = current[q] + volume[q]
        beside = dot(faces_high, near_w[...]) + dot(faces_low, near_w[...])

        for d in range(8):
            pl.when(exists[d])(copies[d].wait_send)
        for d in FAR_FIRST[::-1]:
            pl.when(exists[7 - d])(copies[d].wait_recv)
        got = jnp.transpose(
            jnp.concatenate([recv_buf[step, d] for d in range(8)], axis=0)
        )
        got_high = got.astype(BF16)
        got_low = (got - got_high.astype(F32)).astype(BF16)
        beside = beside + dot(got_high, take_w[...]) + dot(got_low, take_w[...])

        turned = []
        for q in range(QUANT):
            block = beside[q * FROWS : (q + 1) * FROWS]
            low = low_of(block)
            right = jnp.concatenate([block, block, low, jnp.zeros((8, FACES), F32)], axis=0)
            each = dot(rot_w[...], right.astype(BF16))
            turned.append(
                jnp.where(
                    orient == 0,
                    each[0:FROWS],
                    jnp.where(orient == 1, each[FROWS : 2 * FROWS], each[2 * FROWS : 3 * FROWS]),
                )
            )

        fluxes = [[] for _ in range(QUANT)]
        for f in range(4):
            here = slice(f * ELEMS, (f + 1) * ELEMS)
            n = [nrm_ref[k, f : f + 1, :] for k in range(3)]
            both = []
            apart = []
            for q in range(QUANT):
                mine = own[f * FROWS : (f + 1) * FROWS, q * ELEMS : (q + 1) * ELEMS]
                theirs = turned[q][:, here]
                both.append(mine + theirs)
                apart.append(mine - theirs)
            half = 0.5 * root * (jnp.abs(n[0]) + jnp.abs(n[1]) + jnp.abs(n[2]))
            u, v, w = both[6:]
            ns = [-0.5 * shear * x for x in n]
            spread = (-0.5 * lame) * (n[0] * u + n[1] * v + n[2] * w)
            over = [-0.5 * inverse * x for x in n]
            xx, yy, zz, xy, yz, xz = both[:6]
            flux = [
                spread + (2.0 * ns[0]) * u,
                spread + (2.0 * ns[1]) * v,
                spread + (2.0 * ns[2]) * w,
                ns[0] * v + ns[1] * u,
                ns[1] * w + ns[2] * v,
                ns[0] * w + ns[2] * u,
                over[0] * xx + over[1] * xy + over[2] * xz,
                over[0] * xy + over[1] * yy + over[2] * yz,
                over[0] * xz + over[1] * yz + over[2] * zz,
            ]
            for q in range(QUANT):
                fluxes[q].append(flux[q] + half * apart[q])
        lifted = dot(
            lift_w[...], stacked([jnp.concatenate(parts, axis=0) for parts in fluxes], 96)
        )
        for q in range(QUANT):
            out_ref[q] = out_ref[q] - lifted[:, q * ELEMS : (q + 1) * ELEMS]


def solution(mesh):
    rows, cols = mesh.shape["prow"], mesh.shape["pcol"]

    def per_device(*args):
        args = list(args)
        args[3] = args[3].transpose(1, 0, 2)
        args[4] = args[4].transpose(2, 0, 1)
        args[6] = args[6].transpose(1, 0)
        args[7] = args[7].reshape(1, ELEMS)
        args[9] = args[9].transpose(1, 0, 2)
        vmem = pl.BlockSpec(memory_space=pltpu.VMEM)
        return pl.pallas_call(
            functools.partial(kernel, rows, cols),
            out_shape=pltpu.VMEM((QUANT, BASIS, ELEMS), F32),
            in_specs=[pl.BlockSpec(memory_space=pltpu.HBM)] * 15,
            out_specs=vmem,
            scratch_shapes=[pltpu.VMEM(x.shape, x.dtype) for x in args]
            + [
                pltpu.SemaphoreType.DMA((15,)),
                pltpu.VMEM((176, 384), F32),
                pltpu.VMEM((176, 3 * KBLOCK), BF16),
                pltpu.VMEM((176, 3 * KBLOCK), BF16),
                pltpu.VMEM((96, 3 * KBLOCK), BF16),
                pltpu.VMEM((BASIS, 288), BF16),
                pltpu.VMEM((80, 80), BF16),
                pltpu.VMEM((FACES, FACES), BF16),
                pltpu.VMEM((8 * SLOTS, FACES), BF16),
                pltpu.VMEM((8 * SLOTS, FACES), BF16),
                pltpu.VMEM((STEPS, 8, SLOTS, WIDE), F32),
                pltpu.VMEM((STEPS, 8, SLOTS, WIDE), F32),
                pltpu.SemaphoreType.DMA((STEPS, 8)),
                pltpu.SemaphoreType.DMA((STEPS, 8)),
            ],
            compiler_params=pltpu.CompilerParams(
                collective_id=0, has_side_effects=True, vmem_limit_bytes=40 * 1024 * 1024
            ),
        )(*[pltpu.with_memory_space_constraint(x, pltpu.HBM) for x in args])

    both = ("prow", "pcol")
    return jax.shard_map(
        per_device,
        mesh=mesh,
        in_specs=(
            P(None, None, both),
            P(),
            P(),
            P(),
            P(),
            P(),
            P(),
            P(both),
            P(None, None, both),
            P(None, None, both),
            P(None, both),
            P(None, both),
            P(None, both),
            P("prow", "pcol", None, None),
            P("prow", "pcol", None, None),
        ),
        out_specs=P(None, None, both),
        check_vma=False,
    )
```
